1024 devices in a mesh: dp: 256 (over z, y, core), space: 4 (over x).
Axes of the slice: x: 4, y: 8, z: 16, core: 2. Of those that a mesh axis runs over, the one named last changes fastest.
Arguments:
- pressure_tokens: bfloat16 [256, 16, 64, 192], P('dp', 'space'), may hold values from -6 to 6
- dw_kernel: float32 [7, 7, 192], replicated, may hold values from -0.875 to 0.875
- norm_gain: float32 [192], replicated, may hold values from 0.5 to 2
- norm_shift: float32 [192], replicated, may hold values from -3 to 3
- w_expand: bfloat16 [768, 192], P('dp'), may hold values from -0.4375 to 0.4375
- w_reduce: bfloat16 [768, 192], P('dp'), may hold values from -0.21875 to 0.21875
- layer_scale: float32 [192], replicated, may hold values from 0.5 to 2
- cotangent: bfloat16 [256, 16, 64, 192], P('dp', 'space'), may hold values from -6 to 6
Outputs:
- block_out: bfloat16 [256, 16, 64, 192], P('dp', 'space')
- grad_tokens: bfloat16 [256, 16, 64, 192], P('dp', 'space')
- grad_kernel: float32 [7, 7, 192], replicated
- grad_gain: float32 [192], replicated
- grad_shift: float32 [192], replicated
- grad_expand: float32 [768, 192], P('dp')
- grad_reduce: float32 [768, 192], P('dp')
- grad_scale: float32 [192], replicated
The draws below stay inside these ranges and needn't reach their ends.
All inputs are finite; a program needn't handle non-finite values.
Results may differ from the reference program's by a relative error of at most 0.0095.
Values may be sent and summed in bfloat16 or wider, within the bound.
No kernel may reach another device: no remote copies, remote signals or barrier semaphores. Data moves between devices by JAX's collectives and lax.ppermute only.
A program may use at most 32 MiB of HBM per device.

```python
import math
import jax
import jax.numpy as jnp
from jax import lax

D = 192
FF = 768
WIDTH = 64
FIELDS = 256
NROWS = 16


def shard_levels(rng, shape, pieces, low, high):
    def one(position, shards_of):
        steps = jax.random.uniform(jax.random.fold_in(jax.random.fold_in(rng, 6), position), (shards_of,), jnp.float32, low / len(pieces), high / len(pieces))
        return jnp.repeat(jnp.exp(steps), shape[position] // shards_of).reshape((-1,) + (1,) * (len(shape) - position - 1))

    loudness = one(*pieces[0])
    for cut in pieces[1:]:
        loudness = loudness * one(*cut)
    return loudness


def scatter_about(key, shape, deviation, limit, split=(), kind=jnp.bfloat16):
    array = deviation * jax.random.normal(key, shape, jnp.float32)
    if split:
        array = array * shard_levels(key, shape, split, -0.22, 0.18)
    return jnp.clip(array, -limit, limit).astype(kind)


def setup_inputs(seed: int = 0) -> dict:
    key_of = jax.random.split(jax.random.key(seed), 9)
    return {
        "pressure_tokens": scatter_about(key_of[0], (FIELDS, NROWS, WIDTH, D), 1.0, 6.0, ((0, 256), (1, 4))),
        "dw_kernel": scatter_about(key_of[1], (7, 7, D), 49 ** -0.5, 0.875, (), jnp.float32),
        "norm_gain": jnp.clip(jnp.exp(jax.random.uniform(key_of[2], (D,), jnp.float32, math.log(0.5), math.log(2.0))), 0.5, 2.0),
        "norm_shift": scatter_about(key_of[3], (D,), 0.5, 3.0, (), jnp.float32),
        "w_expand": scatter_about(key_of[4], (FF, D), D ** -0.5, 0.4375, ((0, 256),)),
        "w_reduce": scatter_about(key_of[5], (FF, D), FF ** -0.5, 0.21875, ((0, 256),)),
        "layer_scale": jnp.clip(jnp.exp(jax.random.uniform(key_of[6], (D,), jnp.float32, math.log(0.5), math.log(2.0))), 0.5, 2.0),
        "cotangent": scatter_about(key_of[7], (FIELDS, NROWS, WIDTH, D), 1.0, 6.0, ((0, 256), (1, 4))),
    }


def depthwise(padded, kernel):
    channels = padded.shape[-1]
    result = lax.conv_general_dilated(padded[None], kernel[:, :, None, :], (1, 1), 'VALID', dimension_numbers=('NHWC', 'HWIO', 'NHWC'), feature_group_count=channels, precision=lax.Precision.HIGHEST)
    return result[0]

def kernel_product(padded, grad):
    channels = padded.shape[-1]
    result = lax.conv_general_dilated(padded[None], grad[:, :, None, :], (1, 1), 'VALID', dimension_numbers=('NHWC', 'HWIO', 'NHWC'), feature_group_count=channels, precision=lax.Precision.HIGHEST)
    return result[0]

def gelu_slope(pre):
    return 0.5 * (1.0 + lax.erf(pre * 0.7071067811865476)) + pre * jnp.exp(-0.5 * pre * pre) * 0.3989422804014327

def reference(pressure_tokens, dw_kernel, norm_gain, norm_shift, w_expand, w_reduce, layer_scale, cotangent):
    rows = pressure_tokens.shape[1]
    cols = pressure_tokens.shape[2]
    width = pressure_tokens.shape[3]
    cells = rows * cols
    hidden_units = w_expand.shape[0]

    def one_field(carry, inputs):
        field, upstream = inputs
        source = field.astype(jnp.float32)
        padded = jnp.pad(source, ((3, 3), (3, 3), (0, 0)))
        mixed = depthwise(padded, dw_kernel)
        centre = mixed - lax.optimization_barrier(jnp.mean(mixed, -1, keepdims=True))
        inv_std = lax.rsqrt(lax.optimization_barrier(jnp.mean(centre * centre, -1, keepdims=True)) + 1e-06)
        normed = centre * inv_std
        normed_bf = (normed * norm_gain + norm_shift).astype(jnp.bfloat16).reshape(cells, width)
        pre = jnp.dot(normed_bf, w_expand.T, preferred_element_type=jnp.float32)
        hidden = jax.nn.gelu(pre, approximate=False).astype(jnp.bfloat16)
        branch = jnp.dot(hidden, w_reduce, preferred_element_type=jnp.float32)
        flat_source = source.reshape(cells, width)
        output = (flat_source + layer_scale * branch).astype(jnp.bfloat16).reshape(rows, cols, width)
        upstream_f = upstream.astype(jnp.float32).reshape(cells, width)
        scale_grad = lax.optimization_barrier(jnp.sum(upstream_f * branch, 0))
        branch_grad = (upstream_f * layer_scale).astype(jnp.bfloat16)
        hidden_grad = jnp.dot(branch_grad, w_reduce.T, preferred_element_type=jnp.float32)
        pre_grad = (hidden_grad * gelu_slope(pre)).astype(jnp.bfloat16)
        reduce_grad = jnp.dot(hidden.T, branch_grad, preferred_element_type=jnp.float32)
        expand_grad = jnp.dot(pre_grad.T, normed_bf, preferred_element_type=jnp.float32)
        normed_grad = jnp.dot(pre_grad, w_expand, preferred_element_type=jnp.float32).reshape(rows, cols, width)
        gain_grad = lax.optimization_barrier(jnp.sum(normed_grad * normed, (0, 1)))
        shift_grad = lax.optimization_barrier(jnp.sum(normed_grad, (0, 1)))
        scaled = normed_grad * norm_gain
        mixed_grad = inv_std * (scaled - lax.optimization_barrier(jnp.mean(scaled, -1, keepdims=True)) - normed * lax.optimization_barrier(jnp.mean(scaled * normed, -1, keepdims=True)))
        kernel_grad = kernel_product(padded, mixed_grad)
        grad_pad = jnp.pad(mixed_grad, ((3, 3), (3, 3), (0, 0)))
        back = depthwise(grad_pad, dw_kernel[::-1, ::-1])
        grad_in = (upstream_f.reshape(rows, cols, width) + back).astype(jnp.bfloat16)
        acc_kernel, acc_gain, acc_shift, acc_scale, acc_expand, acc_reduce = carry
        carry = (acc_kernel + kernel_grad, acc_gain + gain_grad, acc_shift + shift_grad, acc_scale + scale_grad, acc_expand + expand_grad, acc_reduce + reduce_grad)
        return (carry, (output, grad_in))
    start = (jnp.zeros((7, 7, width), jnp.float32), jnp.zeros((width,), jnp.float32), jnp.zeros((width,), jnp.float32), jnp.zeros((width,), jnp.float32), jnp.zeros((hidden_units, width), jnp.float32), jnp.zeros((hidden_units, width), jnp.float32))
    sums, stacked = lax.scan(one_field, start, (pressure_tokens, cotangent))
    kernel_sum, gain_sum, shift_sum, scale_sum, expand_sum, reduce_sum = sums
    return (stacked[0], stacked[1], kernel_sum, gain_sum, shift_sum, expand_sum, reduce_sum, scale_sum)
```

```python
import jax
import jax.numpy as jnp
from jax import lax
from jax.sharding import Mesh, PartitionSpec as P

DEPTH, HEIGHT, CORES = 16, 8, 2
DP = ("z", "y", "core")


def padded_2(block, dim, width):
    count = lax.axis_size("space")
    forward = [(i, i + 1) for i in range(count - 1)]
    backward = [(target, source) for source, target in forward]
    low = lax.ppermute(
        lax.slice_in_dim(block, block.shape[dim] - width, None, axis=dim), "space", forward
    )
    high = lax.ppermute(lax.slice_in_dim(block, 0, width, axis=dim), "space", backward)
    return jnp.concatenate([low, block, high], axis=dim)


def depthwise(padded, kernel):
    channels = padded.shape[-1]
    result = lax.conv_general_dilated(
        padded[None],
        kernel[:, :, None, :],
        (1, 1),
        "VALID",
        dimension_numbers=("NHWC", "HWIO", "NHWC"),
        feature_group_count=channels,
        precision=lax.Precision.HIGHEST,
    )
    return result[0]


def kernel_product(padded, grad):
    channels = padded.shape[-1]
    result = lax.conv_general_dilated(
        padded[None],
        grad[:, :, None, :],
        (1, 1),
        "VALID",
        dimension_numbers=("NHWC", "HWIO", "NHWC"),
        feature_group_count=channels,
        precision=lax.Precision.HIGHEST,
    )
    return result[0]


def gelu_slope(pre):
    return (
        0.5 * (1.0 + lax.erf(pre * 0.7071067811865476))
        + pre * jnp.exp(-0.5 * pre * pre) * 0.3989422804014327
    )


def other_core(x):
    return lax.ppermute(x, "core", [(0, 1), (1, 0)])


def spread(x, axes, count):
    copies = jnp.broadcast_to(x[None], (count,) + x.shape)
    return lax.all_to_all(copies, axes, 0, 0, tiled=True)


def gather_weights(w_expand, w_reduce):
    block = jnp.concatenate([w_expand, w_reduce], 1)
    units, lanes = block.shape
    column = spread(block, "z", DEPTH).reshape(DEPTH * units, lanes)
    plane = spread(column, "y", HEIGHT).reshape(HEIGHT * DEPTH * units, lanes)
    return jnp.concatenate([plane, other_core(plane)], 0)


def reduce_all(weight_grad, smalls):
    half, lanes = weight_grad.shape[0] // 2, weight_grad.shape[1]
    quarters = lax.axis_size("space")
    part = lanes // quarters
    peers = HEIGHT * quarters
    units = half // (HEIGHT * DEPTH)
    count = smalls.size
    rows = -(-count // (peers * part))
    flat = jnp.pad(smalls.reshape(-1), (0, peers * rows * part - count))
    small_parts = flat.reshape(peers, rows, part)

    def pieces(grad):
        cut = grad.reshape(HEIGHT, DEPTH * units, quarters, part).transpose(0, 2, 1, 3)
        return jnp.concatenate([cut.reshape(peers, DEPTH * units, part), small_parts], 1)

    mine, theirs = pieces(weight_grad[:half]), pieces(weight_grad[half:])
    sums = (mine + other_core(theirs)).astype(jnp.bfloat16)
    arrived = lax.all_to_all(sums, ("y", "space"), 0, 0, tiled=True)
    total = jnp.sum(arrived.astype(jnp.float32), 0)
    column = jnp.concatenate(
        [
            total[: DEPTH * units].reshape(DEPTH, units, part),
            jnp.broadcast_to(total[None, DEPTH * units :], (DEPTH, rows, part)),
        ],
        1,
    )
    total = jnp.sum(lax.all_to_all(column, "z", 0, 0, tiled=True), 0)
    done = spread(total, ("y", "space"), peers)
    own = lax.dynamic_slice_in_dim(done, lax.axis_index("y") * quarters, quarters, 0)
    weight_share = own[:, :units].transpose(1, 0, 2).reshape(units, lanes)
    return weight_share, done[:, units:].reshape(-1)[:count].reshape(smalls.shape)


def shards(
    pressure_tokens, dw_kernel, norm_gain, norm_shift, w_expand, w_reduce, layer_scale, cotangent
):
    rows = pressure_tokens.shape[1]
    cols = pressure_tokens.shape[2]
    width = pressure_tokens.shape[3]
    cells = rows * cols
    extended = padded_2(pressure_tokens, 1, 3)
    weights = gather_weights(w_expand, w_reduce)
    expand, reduce = weights[:, :width], weights[:, width:]
    padded = jnp.pad(extended[0].astype(jnp.float32), ((0, 0), (3, 3), (0, 0)))
    source = padded[3 : 3 + rows, 3 : 3 + cols]
    mixed = depthwise(padded, dw_kernel)
    centre = mixed - jnp.mean(mixed, -1, keepdims=True)
    inv_std = lax.rsqrt(jnp.mean(centre * centre, -1, keepdims=True) + 1e-06)
    normed = centre * inv_std
    normed_bf = (normed * norm_gain + norm_shift).astype(jnp.bfloat16).reshape(cells, width)
    pre = lax.dot_general(
        normed_bf, expand, (((1,), (1,)), ((), ())), preferred_element_type=jnp.float32
    )
    hidden = jax.nn.gelu(pre, approximate=False).astype(jnp.bfloat16)
    branch = jnp.dot(hidden, reduce, preferred_element_type=jnp.float32)
    flat_source = source.reshape(cells, width)
    block_out = (
        (flat_source + layer_scale * branch).astype(jnp.bfloat16).reshape(1, rows, cols, width)
    )
    upstream_f = cotangent[0].astype(jnp.float32).reshape(cells, width)
    scale_grad = jnp.sum(upstream_f * branch, 0)
    branch_grad = (upstream_f * layer_scale).astype(jnp.bfloat16)
    hidden_grad = lax.dot_general(
        branch_grad, reduce, (((1,), (1,)), ((), ())), preferred_element_type=jnp.float32
    )
    pre_grad = (hidden_grad * gelu_slope(pre)).astype(jnp.bfloat16)
    normed_grad = jnp.dot(pre_grad, expand, preferred_element_type=jnp.float32)
    normed_grad = normed_grad.reshape(rows, cols, width)
    gain_grad = jnp.sum(normed_grad * normed, (0, 1))
    shift_grad = jnp.sum(normed_grad, (0, 1))
    scaled = normed_grad * norm_gain
    mixed_grad = inv_std * (
        scaled
        - jnp.mean(scaled, -1, keepdims=True)
        - normed * jnp.mean(scaled * normed, -1, keepdims=True)
    )
    kernel_grad = kernel_product(padded, mixed_grad)
    grad_ext = padded_2(mixed_grad.astype(jnp.bfloat16), 0, 3).astype(mixed_grad.dtype)
    grad_pad = jnp.pad(grad_ext, ((0, 0), (3, 3), (0, 0)))
    back = depthwise(grad_pad, dw_kernel[::-1, ::-1])
    grad_tokens = (
        (upstream_f.reshape(rows, cols, width) + back)
        .astype(jnp.bfloat16)
        .reshape(1, rows, cols, width)
    )
    expand_term = lax.dot_general(
        pre_grad, normed_bf, (((0,), (0,)), ((), ())), preferred_element_type=jnp.float32
    )
    reduce_term = lax.dot_general(
        hidden, branch_grad, (((0,), (0,)), ((), ())), preferred_element_type=jnp.float32
    )
    smalls = jnp.concatenate(
        [kernel_grad.reshape(-1, width), jnp.stack([gain_grad, shift_grad, scale_grad])], 0
    )
    weight_share, smalls = reduce_all(jnp.concatenate([expand_term, reduce_term], 1), smalls)
    taps = kernel_grad.shape[0] * kernel_grad.shape[1]
    return (
        block_out,
        grad_tokens,
        smalls[:taps].reshape(kernel_grad.shape),
        smalls[taps],
        smalls[taps + 1],
        weight_share[:, :width],
        weight_share[:, width:],
        smalls[taps + 2],
    )


def solution(mesh):
    grid = Mesh(
        mesh.devices.reshape(DEPTH, HEIGHT, CORES, mesh.shape["space"]), DP + ("space",)
    )
    tokens, units = P(DP, "space", None, None), P(DP, None)
    in_specs = (tokens, P(), P(), P(), units, units, P(), tokens)
    out_specs = (tokens, tokens, P(), P(), P(), units, units, P())
    return jax.shard_map(shards, mesh=grid, in_specs=in_specs, out_specs=out_specs, check_vma=False)
```

```python
import jax
import jax.numpy as jnp
from jax import lax
from jax.experimental import pallas as pl
from jax.experimental.pallas import tpu as pltpu
from jax.sharding import Mesh, PartitionSpec as P

DEPTH, HEIGHT, CORES, QUARTERS = 16, 8, 2, 4
DP = ("z", "y", "core")
PEERS = HEIGHT * QUARTERS
ROWS, COLS, WIDTH, TAPS = 4, 64, 192, 7
CELLS = ROWS * COLS
HALO = TAPS // 2
PART = WIDTH // 2
UNITS = 3
HALF = HEIGHT * DEPTH * UNITS
BLOCK = DEPTH * UNITS
MARGIN = 8
F32, BF16 = jnp.float32, jnp.bfloat16
SMALL_ROWS = 4


def kernel_call(body, outs, scratch=(), name=None, cost=None):
    return pl.pallas_call(
        body,
        out_shape=[jax.ShapeDtypeStruct(shape, kind) for shape, kind in outs],
        scratch_shapes=list(scratch),
        compiler_params=pltpu.CompilerParams(vmem_limit_bytes=40 * 2**20),
        name=name,
        cost_estimate=cost,
    )


def dot(a, b):
    return jnp.dot(a, b, preferred_element_type=F32)


def dot_rows(a, b):
    return lax.dot_general(a, b, (((0,), (0,)), ((), ())), preferred_element_type=F32)


def fill_padded(padded, low, block, high):
    padded[:, :MARGIN, :] = jnp.zeros((ROWS + 2 * HALO, MARGIN, WIDTH), F32)
    padded[:, MARGIN + COLS :, :] = jnp.zeros((ROWS + 2 * HALO, MARGIN, WIDTH), F32)
    inside = slice(MARGIN, MARGIN + COLS)
    padded[:HALO, inside, :] = low[...].astype(F32)
    padded[HALO : HALO + ROWS, inside, :] = block[...].astype(F32)
    padded[HALO + ROWS :, inside, :] = high[...].astype(F32)


def convolve(padded, tap, finish):
    chunk = 32
    for start in range(0, COLS, chunk):
        acc = [None] * ROWS
        for i in range(ROWS + 2 * HALO):
            for b in range(TAPS):
                first = MARGIN - HALO + b + start
                shifted = padded[i, first : first + chunk, :]
                for r in range(ROWS):
                    if 0 <= i - r < TAPS:
                        term = shifted * tap(i - r, b)
                        acc[r] = term if acc[r] is None else acc[r] + term
        for r in range(ROWS):
            finish(r, start, chunk, acc[r])


def forward_kernel(
    tokens, low, high, taps, gain, shift, scale, cotangent,
    padded, normed, inv_std, norm_halves, norm_t, up_halves, up_t, mixed,
):
    fill_padded(padded, low, tokens, high)

    def finish(r, start, chunk, value):
        mixed[r * COLS + start : r * COLS + start + chunk, :] = value

    convolve(padded, lambda a, b: taps[a, b : b + 1, :], finish)
    value = mixed[...]
    centre = value - jnp.mean(value, -1, keepdims=True)
    inv = lax.rsqrt(jnp.mean(centre * centre, -1, keepdims=True) + 1e-06)
    norm = centre * inv
    normed[...] = norm
    inv_std[...] = inv
    rounded = (norm * gain[...] + shift[...]).astype(BF16)
    upstream = (cotangent[...].reshape(CELLS, WIDTH).astype(F32) * scale[...]).astype(BF16)
    for h in range(2):
        norm_halves[h] = rounded[:, h * PART : (h + 1) * PART]
        up_halves[h] = upstream[:, h * PART : (h + 1) * PART]
    norm_t[...] = rounded.T
    up_t[...] = upstream.T


def main_kernel(
    own, other, tokens, cotangent, padded, normed, inv_std, norm_halves, norm_t, up_halves, up_t,
    gain, scale, mine, theirs, block_out, mixed_grad, smalls, grad_rows,
):
    branch = jnp.zeros((CELLS, WIDTH), F32)
    normed_grad = jnp.zeros((CELLS, WIDTH), F32)
    for weights, out in ((other, theirs), (own, mine)):
        expand, reduce = weights[:, :WIDTH], weights[:, WIDTH:]
        pre = dot(expand, norm_t[...])
        hidden_grad = dot(reduce, up_t[...])
        cumulative = 0.5 * (1.0 + lax.erf(pre * 0.7071067811865476))
        hidden = (pre * cumulative).astype(BF16)
        slope = cumulative + pre * jnp.exp(-0.5 * pre * pre) * 0.3989422804014327
        pre_grad = (hidden_grad * slope).astype(BF16)
        for q in range(QUARTERS):
            left, right = (pre_grad, norm_halves) if q < 2 else (hidden, up_halves)
            grad = dot(left, right[q % 2])
            for y in range(HEIGHT):
                base = y * BLOCK
                piece = y * QUARTERS + q
                out[piece, 0:40, 0:PART] = grad[base : base + 40]
                tail = grad[base + 40 : base + 48]
                for k in range(3):
                    out[piece, 8 * k : 8 * k + 8, PART:128] = tail[:, 32 * k : 32 * k + 32]
        branch += dot_rows(hidden, reduce)
        normed_grad += dot_rows(pre_grad, expand)
    flat = tokens[...].reshape(CELLS, WIDTH).astype(F32)
    block_out[...] = (flat + scale[...] * branch).astype(BF16).reshape(ROWS, COLS, WIDTH)
    norm = normed[...]
    upstream = cotangent[...].reshape(CELLS, WIDTH).astype(F32)
    smalls[TAPS * TAPS :, :] = jnp.zeros((64 - TAPS * TAPS, WIDTH), F32)
    smalls[49:50, :] = jnp.sum(normed_grad * norm, 0, keepdims=True)
    smalls[50:51, :] = jnp.sum(normed_grad, 0, keepdims=True)
    smalls[51:52, :] = jnp.sum(upstream * branch, 0, keepdims=True)
    scaled = normed_grad * gain[...]
    grad = inv_std[...] * (
        scaled
        - jnp.mean(scaled, -1, keepdims=True)
        - norm * jnp.mean(scaled * norm, -1, keepdims=True)
    )
    grad_rows[...] = grad.reshape(ROWS, COLS, WIDTH)
    mixed_grad[...] = grad.astype(BF16).reshape(ROWS, COLS, WIDTH)
    for b in range(TAPS):
        acc = [None] * TAPS
        for i in range(ROWS + 2 * HALO):
            first = MARGIN - HALO + b
            shifted = padded[i, first : first + COLS, :]
            for r in range(ROWS):
                a = i - r
                if 0 <= a < TAPS:
                    product = (shifted * grad_rows[r]).reshape(COLS // 8, 8, WIDTH)
                    term = jnp.sum(product, 0)
                    acc[a] = term if acc[a] is None else acc[a] + term
        for a in range(TAPS):
            row = a * TAPS + b
            smalls[row : row + 1, :] = jnp.sum(acc[a], 0, keepdims=True)
    for piece in range(PEERS):
        row = SMALL_ROWS * (piece % 16)
        lane = PART * (piece // 16)
        values = smalls[row : row + SMALL_ROWS, lane : lane + PART]
        for out in (mine, theirs):
            for k in range(3):
                at = 24 + SMALL_ROWS * k
                out[piece, at : at + SMALL_ROWS, PART:128] = values[:, 32 * k : 32 * k + 32]
            out[piece, 36:40, PART:128] = jnp.zeros((4, 32), F32)


def middle_kernel(arrived, column):
    total = arrived[0].astype(F32)
    for p in range(1, PEERS):
        total += arrived[p].astype(F32)
    tail = jnp.concatenate([total[8 * k : 8 * k + 8, PART:128] for k in range(3)], 1)
    grad = jnp.concatenate([total[:, :PART], tail], 0)
    at = [24 + SMALL_ROWS * k for k in range(3)]
    small = jnp.concatenate([total[i : i + SMALL_ROWS, PART:128] for i in at], 1)
    for z in range(DEPTH):
        column[z, 0:UNITS, :] = grad[z * UNITS : (z + 1) * UNITS]
        column[z, UNITS : UNITS + SMALL_ROWS, :] = small
        column[z, UNITS + SMALL_ROWS :, :] = jnp.zeros((1, PART), F32)


def spread_kernel(arrived, copies):
    total = jnp.sum(arrived[...], 0)
    for p in range(PEERS):
        copies[p] = total


def final_kernel(height, done, kernel_grad, gain_grad, shift_grad, scale_grad, expand, reduce):
    y = height[0]
    for q in range(QUARTERS):
        out = expand if q < 2 else reduce
        out[:, (q % 2) * PART : (q % 2 + 1) * PART] = done[y * QUARTERS + q, 0:UNITS, :]
    for row in range(TAPS * TAPS + 3):
        p, i = row // SMALL_ROWS, UNITS + row % SMALL_ROWS
        value = jnp.concatenate([done[p, i : i + 1, :], done[16 + p, i : i + 1, :]], 1)
        if row < TAPS * TAPS:
            kernel_grad[row // TAPS, row % TAPS : row % TAPS + 1, :] = value
        else:
            (gain_grad, shift_grad, scale_grad)[row - TAPS * TAPS][...] = value


def backward_kernel(grad, low, high, taps, cotangent, out, padded):
    fill_padded(padded, low, grad, high)

    def finish(r, start, chunk, value):
        upstream = cotangent[r, start : start + chunk, :].astype(F32)
        out[r, start : start + chunk, :] = (upstream + value).astype(BF16)

    convolve(padded, lambda a, b: taps[TAPS - 1 - a, TAPS - 1 - b : TAPS - b, :], finish)


def neighbours(block):
    forward = [(i, i + 1) for i in range(QUARTERS - 1)]
    backward = [(target, source) for source, target in forward]
    low = lax.ppermute(block[ROWS - HALO :], "space", forward)
    high = lax.ppermute(block[:HALO], "space", backward)
    return low, high


def other_core(x):
    return lax.ppermute(x, "core", [(0, 1), (1, 0)])


def exchange(x, axes):
    return lax.all_to_all(x, axes, 0, 0, tiled=True)


def shards(
    pressure_tokens, dw_kernel, norm_gain, norm_shift, w_expand, w_reduce, layer_scale, cotangent
):
    tokens, upstream = pressure_tokens[0], cotangent[0]
    gain, shift, scale = norm_gain[None], norm_shift[None], layer_scale[None]

    def copies(x):
        return jnp.broadcast_to(x[None], (DEPTH,) + x.shape)

    column = exchange(jnp.concatenate([copies(w_expand), copies(w_reduce)], 2), "z")
    column, tokens = lax.optimization_barrier((column, tokens))
    plane = column.reshape(1, BLOCK, 2 * WIDTH)
    own = exchange(jnp.broadcast_to(plane, (HEIGHT, BLOCK, 2 * WIDTH)), "y")
    low, high = neighbours(tokens)
    padded, normed, inv_std, norm_halves, norm_t, up_halves, up_t = kernel_call(
        forward_kernel,
        [
            ((ROWS + 2 * HALO, COLS + 2 * MARGIN, WIDTH), F32),
            ((CELLS, WIDTH), F32),
            ((CELLS, 1), F32),
            ((2, CELLS, PART), BF16),
            ((WIDTH, CELLS), BF16),
            ((2, CELLS, PART), BF16),
            ((WIDTH, CELLS), BF16),
        ],
        [pltpu.VMEM((CELLS, WIDTH), F32)],
        "forward",
        pl.CostEstimate(flops=8_000_000, bytes_accessed=2_000_000, transcendentals=256),
    )(tokens, low, high, dw_kernel, gain, shift, scale, upstream)
    own = own.reshape(HALF, 2 * WIDTH)
    other = other_core(own)
    mine, theirs, block_out, mixed_grad = kernel_call(
        main_kernel,
        [
            ((PEERS, 40, 128), F32),
            ((PEERS, 40, 128), F32),
            ((ROWS, COLS, WIDTH), BF16),
            ((ROWS, COLS, WIDTH), BF16),
        ],
        [pltpu.VMEM((64, WIDTH), F32), pltpu.VMEM((ROWS, COLS, WIDTH), F32)],
        "main",
        pl.CostEstimate(flops=500_000_000, bytes_accessed=4_000_000, transcendentals=400_000),
    )(
        own, other, tokens, upstream, padded, normed, inv_std, norm_halves, norm_t, up_halves,
        up_t, gain, scale,
    )
    sums = (mine + other_core(theirs)).astype(BF16)
    sums, mixed_grad = lax.optimization_barrier((sums, mixed_grad))
    arrived = exchange(sums, ("y", "space"))
    grad_low, grad_high = neighbours(mixed_grad)
    (column,) = kernel_call(middle_kernel, [((DEPTH, 8, PART), F32)], name="middle")(arrived)
    column = exchange(column, "z")
    column, mixed_grad, grad_low, grad_high = lax.optimization_barrier(
        (column, mixed_grad, grad_low, grad_high)
    )
    (spread,) = kernel_call(spread_kernel, [((PEERS, 8, PART), F32)], name="spread")(column)
    done = exchange(spread, ("y", "space"))
    (grad_tokens,) = kernel_call(
        backward_kernel,
        [((ROWS, COLS, WIDTH), BF16)],
        [pltpu.VMEM((ROWS + 2 * HALO, COLS + 2 * MARGIN, WIDTH), F32)],
        "backward",
        pl.CostEstimate(flops=8_000_000, bytes_accessed=1_000_000, transcendentals=0),
    )(mixed_grad, grad_low, grad_high, dw_kernel, upstream)
    kernel_grad, gain_grad, shift_grad, scale_grad, grad_expand, grad_reduce = pl.pallas_call(
        final_kernel,
        out_shape=[
            jax.ShapeDtypeStruct(shape, F32)
            for shape in [(TAPS, TAPS, WIDTH)] + [(1, WIDTH)] * 3 + [(UNITS, WIDTH)] * 2
        ],
        in_specs=[
            pl.BlockSpec(memory_space=pltpu.SMEM),
            pl.BlockSpec(memory_space=pltpu.VMEM),
        ],
        compiler_params=pltpu.CompilerParams(vmem_limit_bytes=40 * 2**20),
        name="final",
    )(lax.axis_index("y").reshape(1), done)
    return (
        block_out[None],
        grad_tokens[None],
        kernel_grad,
        gain_grad[0],
        shift_grad[0],
        grad_expand,
        grad_reduce,
        scale_grad[0],
    )


def solution(mesh):
    grid = Mesh(mesh.devices.reshape(DEPTH, HEIGHT, CORES, QUARTERS), DP + ("space",))
    tokens, units = P(DP, "space", None, None), P(DP, None)
    in_specs = (tokens, P(), P(), P(), units, units, P(), tokens)
    out_specs = (tokens, tokens, P(), P(), P(), units, units, P())
    return jax.shard_map(shards, mesh=grid, in_specs=in_specs, out_specs=out_specs, check_vma=False)
```

```python
import jax
import jax.numpy as jnp
from jax import lax
from jax.experimental import pallas as pl
from jax.experimental.pallas import tpu as pltpu
from jax.sharding import Mesh, PartitionSpec as P

DEPTH, HEIGHT, CORES, QUARTERS = 16, 8, 2, 4
DP = ("z", "y", "core")
PEERS = HEIGHT * QUARTERS
ROWS, COLS, WIDTH, TAPS = 4, 64, 192, 7
CELLS = ROWS * COLS
HALO = TAPS // 2
PART = WIDTH // 2
UNITS = 3
HALF = HEIGHT * DEPTH * UNITS
BLOCK = DEPTH * UNITS
MARGIN = 8
F32, BF16 = jnp.float32, jnp.bfloat16
SMALL_ROWS = 4


def kernel_call(body, outs, scratch=(), name=None, cost=None):
    return pl.pallas_call(
        body,
        out_shape=[jax.ShapeDtypeStruct(shape, kind) for shape, kind in outs],
        scratch_shapes=list(scratch),
        compiler_params=pltpu.CompilerParams(vmem_limit_bytes=40 * 2**20),
        name=name,
        cost_estimate=cost,
    )


def dot(a, b):
    return jnp.dot(a, b, preferred_element_type=F32)


def dot_rows(a, b):
    return lax.dot_general(a, b, (((0,), (0,)), ((), ())), preferred_element_type=F32)


def fill_padded(padded, low, block, high):
    padded[:, :MARGIN, :] = jnp.zeros((ROWS + 2 * HALO, MARGIN, WIDTH), F32)
    padded[:, MARGIN + COLS :, :] = jnp.zeros((ROWS + 2 * HALO, MARGIN, WIDTH), F32)
    inside = slice(MARGIN, MARGIN + COLS)
    padded[:HALO, inside, :] = low[...].astype(F32)
    padded[HALO : HALO + ROWS, inside, :] = block[...].astype(F32)
    padded[HALO + ROWS :, inside, :] = high[...].astype(F32)


def convolve(padded, tap, finish):
    chunk = 32
    for start in range(0, COLS, chunk):
        acc = [None] * ROWS
        for i in range(ROWS + 2 * HALO):
            for b in range(TAPS):
                first = MARGIN - HALO + b + start
                shifted = padded[i, first : first + chunk, :]
                for r in range(ROWS):
                    if 0 <= i - r < TAPS:
                        term = shifted * tap(i - r, b)
                        acc[r] = term if acc[r] is None else acc[r] + term
        for r in range(ROWS):
            finish(r, start, chunk, acc[r])


def forward_kernel(
    tokens, low, high, taps, gain, shift, scale, cotangent,
    padded, normed, inv_std, norm_halves, norm_t, up_halves, up_t, mixed,
):
    fill_padded(padded, low, tokens, high)

    def finish(r, start, chunk, value):
        mixed[r * COLS + start : r * COLS + start + chunk, :] = value

    convolve(padded, lambda a, b: taps[a, b : b + 1, :], finish)
    value = mixed[...]
    centre = value - jnp.mean(value, -1, keepdims=True)
    inv = lax.rsqrt(jnp.mean(centre * centre, -1, keepdims=True) + 1e-06)
    norm = centre * inv
    normed[...] = norm
    inv_std[...] = inv
    rounded = (norm * gain[...] + shift[...]).astype(BF16)
    upstream = (cotangent[...].reshape(CELLS, WIDTH).astype(F32) * scale[...]).astype(BF16)
    for h in range(2):
        norm_halves[h] = rounded[:, h * PART : (h + 1) * PART]
        up_halves[h] = upstream[:, h * PART : (h + 1) * PART]
    norm_t[...] = rounded.T
    up_t[...] = upstream.T


def main_kernel(
    own, other, tokens, cotangent, padded, normed, inv_std, norm_halves, norm_t, up_halves, up_t,
    gain, scale, mine, theirs_bf, block_out, mixed_grad, smalls, grad_rows, theirs,
):
    branch = jnp.zeros((CELLS, WIDTH), F32)
    normed_grad = jnp.zeros((CELLS, WIDTH), F32)
    for weights, out in ((other, theirs), (own, mine)):
        expand, reduce = weights[:, :WIDTH], weights[:, WIDTH:]
        pre = dot(expand, norm_t[...])
        hidden_grad = dot(reduce, up_t[...])
        cumulative = 0.5 * (1.0 + lax.erf(pre * 0.7071067811865476))
        hidden = (pre * cumulative).astype(BF16)
        slope = cumulative + pre * jnp.exp(-0.5 * pre * pre) * 0.3989422804014327
        pre_grad = (hidden_grad * slope).astype(BF16)
        for q in range(QUARTERS):
            left, right = (pre_grad, norm_halves) if q < 2 else (hidden, up_halves)
            grad = dot(left, right[q % 2])
            for y in range(HEIGHT):
                base = y * BLOCK
                piece = y * QUARTERS + q
                out[piece, 0:40, 0:PART] = grad[base : base + 40]
                tail = grad[base + 40 : base + 48]
                for k in range(3):
                    out[piece, 8 * k : 8 * k + 8, PART:128] = tail[:, 32 * k : 32 * k + 32]
        branch += dot_rows(hidden, reduce)
        normed_grad += dot_rows(pre_grad, expand)
    flat = tokens[...].reshape(CELLS, WIDTH).astype(F32)
    block_out[...] = (flat + scale[...] * branch).astype(BF16).reshape(ROWS, COLS, WIDTH)
    norm = normed[...]
    upstream = cotangent[...].reshape(CELLS, WIDTH).astype(F32)
    smalls[TAPS * TAPS :, :] = jnp.zeros((64 - TAPS * TAPS, WIDTH), F32)
    smalls[49:50, :] = jnp.sum(normed_grad * norm, 0, keepdims=True)
    smalls[50:51, :] = jnp.sum(normed_grad, 0, keepdims=True)
    smalls[51:52, :] = jnp.sum(upstream * branch, 0, keepdims=True)
    scaled = normed_grad * gain[...]
    grad = inv_std[...] * (
        scaled
        - jnp.mean(scaled, -1, keepdims=True)
        - norm * jnp.mean(scaled * norm, -1, keepdims=True)
    )
    grad_rows[...] = grad.reshape(ROWS, COLS, WIDTH)
    mixed_grad[...] = grad.astype(BF16).reshape(ROWS, COLS, WIDTH)
    for b in range(TAPS):
        acc = [None] * TAPS
        for i in range(ROWS + 2 * HALO):
            first = MARGIN - HALO + b
            shifted = padded[i, first : first + COLS, :]
            for r in range(ROWS):
                a = i - r
                if 0 <= a < TAPS:
                    product = (shifted * grad_rows[r]).reshape(COLS // 8, 8, WIDTH)
                    term = jnp.sum(product, 0)
                    acc[a] = term if acc[a] is None else acc[a] + term
        for a in range(TAPS):
            row = a * TAPS + b
            smalls[row : row + 1, :] = jnp.sum(acc[a], 0, keepdims=True)
    for piece in range(PEERS):
        row = SMALL_ROWS * (piece % 16)
        lane = PART * (piece // 16)
        values = smalls[row : row + SMALL_ROWS, lane : lane + PART]
        for out in (mine, theirs):
            for k in range(3):
                at = 24 + SMALL_ROWS * k
                out[piece, at : at + SMALL_ROWS, PART:128] = values[:, 32 * k : 32 * k + 32]
            out[piece, 36:40, PART:128] = jnp.zeros((4, 32), F32)
    theirs_bf[...] = theirs[...].astype(BF16)


def middle_kernel(arrived, column):
    total = arrived[0].astype(F32)
    for p in range(1, PEERS):
        total += arrived[p].astype(F32)
    tail = jnp.concatenate([total[8 * k : 8 * k + 8, PART:128] for k in range(3)], 1)
    grad = jnp.concatenate([total[:, :PART], tail], 0)
    at = [24 + SMALL_ROWS * k for k in range(3)]
    small = jnp.concatenate([total[i : i + SMALL_ROWS, PART:128] for i in at], 1)
    for z in range(DEPTH):
        column[z, 0:UNITS, :] = grad[z * UNITS : (z + 1) * UNITS]
        column[z, UNITS : UNITS + SMALL_ROWS, :] = small
        column[z, UNITS + SMALL_ROWS :, :] = jnp.zeros((1, PART), F32)


def spread_kernel(arrived, copies):
    total = jnp.sum(arrived[...], 0)
    for p in range(PEERS):
        copies[p] = total


def final_kernel(height, done, kernel_grad, gain_grad, shift_grad, scale_grad, expand, reduce):
    y = height[0]
    for q in range(QUARTERS):
        out = expand if q < 2 else reduce
        out[:, (q % 2) * PART : (q % 2 + 1) * PART] = done[y * QUARTERS + q, 0:UNITS, :]
    for row in range(TAPS * TAPS + 3):
        p, i = row // SMALL_ROWS, UNITS + row % SMALL_ROWS
        value = jnp.concatenate([done[p, i : i + 1, :], done[16 + p, i : i + 1, :]], 1)
        if row < TAPS * TAPS:
            kernel_grad[row // TAPS, row % TAPS : row % TAPS + 1, :] = value
        else:
            (gain_grad, shift_grad, scale_grad)[row - TAPS * TAPS][...] = value


def backward_kernel(grad, low, high, taps, cotangent, out, padded):
    fill_padded(padded, low, grad, high)

    def finish(r, start, chunk, value):
        upstream = cotangent[r, start : start + chunk, :].astype(F32)
        out[r, start : start + chunk, :] = (upstream + value).astype(BF16)

    convolve(padded, lambda a, b: taps[TAPS - 1 - a, TAPS - 1 - b : TAPS - b, :], finish)


def neighbours(block):
    forward = [(i, i + 1) for i in range(QUARTERS - 1)]
    backward = [(target, source) for source, target in forward]
    low = lax.ppermute(block[ROWS - HALO :], "space", forward)
    high = lax.ppermute(block[:HALO], "space", backward)
    return low, high


def other_core(x):
    return lax.ppermute(x, "core", [(0, 1), (1, 0)])


def exchange(x, axes):
    return lax.all_to_all(x, axes, 0, 0, tiled=True)


def shards(
    pressure_tokens, dw_kernel, norm_gain, norm_shift, w_expand, w_reduce, layer_scale, cotangent
):
    tokens, upstream = pressure_tokens[0], cotangent[0]
    gain, shift, scale = norm_gain[None], norm_shift[None], layer_scale[None]

    def copies(x):
        return jnp.broadcast_to(x[None], (DEPTH,) + x.shape)

    column = exchange(jnp.concatenate([copies(w_expand), copies(w_reduce)], 2), "z")
    column, tokens = lax.optimization_barrier((column, tokens))
    plane = column.reshape(1, BLOCK, 2 * WIDTH)
    own = exchange(jnp.broadcast_to(plane, (HEIGHT, BLOCK, 2 * WIDTH)), "y")
    low, high = neighbours(tokens)
    padded, normed, inv_std, norm_halves, norm_t, up_halves, up_t = kernel_call(
        forward_kernel,
        [
            ((ROWS + 2 * HALO, COLS + 2 * MARGIN, WIDTH), F32),
            ((CELLS, WIDTH), F32),
            ((CELLS, 1), F32),
            ((2, CELLS, PART), BF16),
            ((WIDTH, CELLS), BF16),
            ((2, CELLS, PART), BF16),
            ((WIDTH, CELLS), BF16),
        ],
        [pltpu.VMEM((CELLS, WIDTH), F32)],
        "forward",
        pl.CostEstimate(flops=8_000_000, bytes_accessed=2_000_000, transcendentals=256),
    )(tokens, low, high, dw_kernel, gain, shift, scale, upstream)
    own, norm_t = lax.optimization_barrier((own, norm_t))
    own = own.reshape(HALF, 2 * WIDTH)
    other = other_core(own)
    mine, theirs, block_out, mixed_grad = kernel_call(
        main_kernel,
        [
            ((PEERS, 40, 128), F32),
            ((PEERS, 40, 128), BF16),
            ((ROWS, COLS, WIDTH), BF16),
            ((ROWS, COLS, WIDTH), BF16),
        ],
        [
            pltpu.VMEM((64, WIDTH), F32),
            pltpu.VMEM((ROWS, COLS, WIDTH), F32),
            pltpu.VMEM((PEERS, 40, 128), F32),
        ],
        "main",
        pl.CostEstimate(flops=500_000_000, bytes_accessed=4_000_000, transcendentals=400_000),
    )(
        own, other, tokens, upstream, padded, normed, inv_std, norm_halves, norm_t, up_halves,
        up_t, gain, scale,
    )
    sums = (mine + other_core(theirs).astype(F32)).astype(BF16)
    sums, mixed_grad = lax.optimization_barrier((sums, mixed_grad))
    arrived = exchange(sums, ("y", "space"))
    grad_low, grad_high = neighbours(mixed_grad)
    (column,) = kernel_call(middle_kernel, [((DEPTH, 8, PART), F32)], name="middle")(arrived)
    column = exchange(column, "z")
    (grad_tokens,) = kernel_call(
        backward_kernel,
        [((ROWS, COLS, WIDTH), BF16)],
        [pltpu.VMEM((ROWS + 2 * HALO, COLS + 2 * MARGIN, WIDTH), F32)],
        "backward",
        pl.CostEstimate(flops=8_000_000, bytes_accessed=1_000_000, transcendentals=0),
    )(mixed_grad, grad_low, grad_high, dw_kernel, upstream)
    height = lax.axis_index("y").reshape(1)
    column, grad_tokens, height = lax.optimization_barrier((column, grad_tokens, height))
    (spread,) = kernel_call(spread_kernel, [((PEERS, 8, PART), F32)], name="spread")(column)
    done = exchange(spread, ("y", "space"))
    kernel_grad, gain_grad, shift_grad, scale_grad, grad_expand, grad_reduce = pl.pallas_call(
        final_kernel,
        out_shape=[
            jax.ShapeDtypeStruct(shape, F32)
            for shape in [(TAPS, TAPS, WIDTH)] + [(1, WIDTH)] * 3 + [(UNITS, WIDTH)] * 2
        ],
        in_specs=[
            pl.BlockSpec(memory_space=pltpu.SMEM),
            pl.BlockSpec(memory_space=pltpu.VMEM),
        ],
        compiler_params=pltpu.CompilerParams(vmem_limit_bytes=40 * 2**20),
        name="final",
    )(height, done)
    return (
        block_out[None],
        grad_tokens[None],
        kernel_grad,
        gain_grad[0],
        shift_grad[0],
        grad_expand,
        grad_reduce,
        scale_grad[0],
    )


def solution(mesh):
    grid = Mesh(mesh.devices.reshape(DEPTH, HEIGHT, CORES, QUARTERS), DP + ("space",))
    tokens, units = P(DP, "space", None, None), P(DP, None)
    in_specs = (tokens, P(), P(), P(), units, units, P(), tokens)
    out_specs = (tokens, tokens, P(), P(), P(), units, units, P())
    return jax.shard_map(shards, mesh=grid, in_specs=in_specs, out_specs=out_specs, check_vma=False)
```

```python
import jax
import jax.numpy as jnp
from jax import lax
from jax.experimental import pallas as pl
from jax.experimental.pallas import tpu as pltpu
from jax.sharding import Mesh, PartitionSpec as P

DEPTH, HEIGHT, CORES, QUARTERS = 16, 8, 2, 4
DP = ("z", "y", "core")
PEERS = HEIGHT * QUARTERS
ROWS, COLS, WIDTH, TAPS = 4, 64, 192, 7
CELLS = ROWS * COLS
HALO = TAPS // 2
PART = WIDTH // 2
UNITS = 3
HALF = HEIGHT * DEPTH * UNITS
BLOCK = DEPTH * UNITS
MARGIN = 8
F32, BF16 = jnp.float32, jnp.bfloat16
SMALL_ROWS = 4
PADDED = (ROWS + 2 * HALO, COLS + 2 * MARGIN, WIDTH)
SHIFTED = (TAPS, ROWS, COLS + 2 * MARGIN, WIDTH)


def kernel_call(body, outs, scratch=(), name=None, cost=None):
    return pl.pallas_call(
        body,
        out_shape=[jax.ShapeDtypeStruct(shape, kind) for shape, kind in outs],
        scratch_shapes=list(scratch),
        compiler_params=pltpu.CompilerParams(vmem_limit_bytes=40 * 2**20),
        name=name,
        cost_estimate=cost,
    )


def dot(a, b):
    return jnp.dot(a, b, preferred_element_type=F32)


def dot_rows(a, b):
    return lax.dot_general(a, b, (((0,), (0,)), ((), ())), preferred_element_type=F32)


def fill_padded(padded, low, block, high):
    padded[:, :MARGIN, :] = jnp.zeros((ROWS + 2 * HALO, MARGIN, WIDTH), F32)
    padded[:, MARGIN + COLS :, :] = jnp.zeros((ROWS + 2 * HALO, MARGIN, WIDTH), F32)
    inside = slice(MARGIN, MARGIN + COLS)
    padded[:HALO, inside, :] = low[...].astype(F32)
    padded[HALO : HALO + ROWS, inside, :] = block[...].astype(F32)
    padded[HALO + ROWS :, inside, :] = high[...].astype(F32)


def convolve(padded, shifted, tap, finish):
    for b in range(TAPS):
        taps_b = [jnp.broadcast_to(tap(a, b), (8, WIDTH)) for a in range(TAPS)]
        for t in range((MARGIN - HALO + b) // 8, (MARGIN - HALO + b + COLS + 7) // 8):
            acc = [None] * ROWS
            for i in range(ROWS + 2 * HALO):
                field = padded[i, 8 * t : 8 * t + 8, :]
                for r in range(ROWS):
                    if 0 <= i - r < TAPS:
                        term = field * taps_b[i - r]
                        acc[r] = term if acc[r] is None else acc[r] + term
            for r in range(ROWS):
                shifted[b, r, 8 * t : 8 * t + 8, :] = acc[r]
    for r in range(ROWS):
        for start in range(0, COLS, 32):
            total = None
            for b in range(TAPS):
                first = MARGIN - HALO + b + start
                value = shifted[b, r, first : first + 32, :]
                total = value if total is None else total + value
            finish(r, start, 32, total)


def forward_kernel(
    tokens, low, high, taps, vectors, cotangent,
    padded, normed, inv_std, norm_halves, norm_t, up_halves, up_t, mixed, shifted,
):
    fill_padded(padded, low, tokens, high)

    def finish(r, start, chunk, value):
        mixed[r * COLS + start : r * COLS + start + chunk, :] = value

    convolve(padded, shifted, lambda a, b: taps[a, b : b + 1, :], finish)
    value = mixed[...]
    centre = value - jnp.mean(value, -1, keepdims=True)
    inv = lax.rsqrt(jnp.mean(centre * centre, -1, keepdims=True) + 1e-06)
    norm = centre * inv
    normed[...] = norm
    inv_std[...] = inv
    rounded = (norm * vectors[0:1] + vectors[1:2]).astype(BF16)
    upstream = (cotangent[...].reshape(CELLS, WIDTH).astype(F32) * vectors[2:3]).astype(BF16)
    for h in range(2):
        norm_halves[h] = rounded[:, h * PART : (h + 1) * PART]
        up_halves[h] = upstream[:, h * PART : (h + 1) * PART]
    norm_t[...] = rounded.T
    up_t[...] = upstream.T


def main_kernel(
    own, other, tokens, cotangent, padded, normed, inv_std, norm_halves, norm_t, up_halves, up_t,
    vectors, mine, theirs_bf, block_out, mixed_grad, smalls, grad_rows, theirs,
):
    branch = jnp.zeros((CELLS, WIDTH), F32)
    normed_grad = jnp.zeros((CELLS, WIDTH), F32)
    for weights, out in ((other, theirs), (own, mine)):
        expand, reduce = weights[:, :WIDTH], weights[:, WIDTH:]
        pre = dot(expand, norm_t[...])
        hidden_grad = dot(reduce, up_t[...])
        cumulative = 0.5 * (1.0 + lax.erf(pre * 0.7071067811865476))
        hidden = (pre * cumulative).astype(BF16)
        slope = cumulative + pre * jnp.exp(-0.5 * pre * pre) * 0.3989422804014327
        pre_grad = (hidden_grad * slope).astype(BF16)
        for q in range(QUARTERS):
            left, right = (pre_grad, norm_halves) if q < 2 else (hidden, up_halves)
            grad = dot(left, right[q % 2])
            for y in range(HEIGHT):
                base = y * BLOCK
                piece = y * QUARTERS + q
                out[piece, 0:40, 0:PART] = grad[base : base + 40]
                tail = grad[base + 40 : base + 48]
                for k in range(3):
                    out[piece, 8 * k : 8 * k + 8, PART:128] = tail[:, 32 * k : 32 * k + 32]
        branch += dot_rows(hidden, reduce)
        normed_grad += dot_rows(pre_grad, expand)
    flat = tokens[...].reshape(CELLS, WIDTH).astype(F32)
    block_out[...] = (flat + vectors[2:3] * branch).astype(BF16).reshape(ROWS, COLS, WIDTH)
    norm = normed[...]
    upstream = cotangent[...].reshape(CELLS, WIDTH).astype(F32)
    smalls[TAPS * TAPS :, :] = jnp.zeros((64 - TAPS * TAPS, WIDTH), F32)
    smalls[49:50, :] = jnp.sum(normed_grad * norm, 0, keepdims=True)
    smalls[50:51, :] = jnp.sum(normed_grad, 0, keepdims=True)
    smalls[51:52, :] = jnp.sum(upstream * branch, 0, keepdims=True)
    scaled = normed_grad * vectors[0:1]
    grad = inv_std[...] * (
        scaled
        - jnp.mean(scaled, -1, keepdims=True)
        - norm * jnp.mean(scaled * norm, -1, keepdims=True)
    )
    grad_rows[:, :MARGIN, :] = jnp.zeros((ROWS, MARGIN, WIDTH), F32)
    grad_rows[:, MARGIN + COLS :, :] = jnp.zeros((ROWS, MARGIN, WIDTH), F32)
    grad_rows[:, MARGIN : MARGIN + COLS, :] = grad.reshape(ROWS, COLS, WIDTH)
    mixed_grad[...] = grad.astype(BF16).reshape(ROWS, COLS, WIDTH)
    for b in range(TAPS):
        acc = [None] * TAPS
        for t in range((MARGIN - HALO + b) // 8, (MARGIN - HALO + b + COLS + 7) // 8):
            first = 8 * t + HALO - b
            grads = [grad_rows[r, first : first + 8, :] for r in range(ROWS)]
            for i in range(ROWS + 2 * HALO):
                field = padded[i, 8 * t : 8 * t + 8, :]
                for r in range(ROWS):
                    a = i - r
                    if 0 <= a < TAPS:
                        term = field * grads[r]
                        acc[a] = term if acc[a] is None else acc[a] + term
        for a in range(TAPS):
            row = a * TAPS + b
            smalls[row : row + 1, :] = jnp.sum(acc[a], 0, keepdims=True)
    for piece in range(PEERS):
        row = SMALL_ROWS * (piece % 16)
        lane = PART * (piece // 16)
        values = smalls[row : row + SMALL_ROWS, lane : lane + PART]
        for out in (mine, theirs):
            for k in range(3):
                at = 24 + SMALL_ROWS * k
                out[piece, at : at + SMALL_ROWS, PART:128] = values[:, 32 * k : 32 * k + 32]
            out[piece, 36:40, PART:128] = jnp.zeros((4, 32), F32)
    theirs_bf[...] = theirs[...].astype(BF16)


def middle_kernel(arrived, column):
    total = arrived[0].astype(F32)
    for p in range(1, PEERS):
        total += arrived[p].astype(F32)
    tail = jnp.concatenate([total[8 * k : 8 * k + 8, PART:128] for k in range(3)], 1)
    grad = jnp.concatenate([total[:, :PART], tail], 0)
    at = [24 + SMALL_ROWS * k for k in range(3)]
    small = jnp.concatenate([total[i : i + SMALL_ROWS, PART:128] for i in at], 1)
    for z in range(DEPTH):
        column[z, 0:UNITS, :] = grad[z * UNITS : (z + 1) * UNITS]
        column[z, UNITS : UNITS + SMALL_ROWS, :] = small
        column[z, UNITS + SMALL_ROWS :, :] = jnp.zeros((1, PART), F32)


def spread_kernel(arrived, copies):
    total = jnp.sum(arrived[...], 0)
    for p in range(PEERS):
        copies[p] = total


def final_kernel(height, done, kernel_grad, gain_grad, shift_grad, scale_grad, expand, reduce):
    y = height[0]
    for q in range(QUARTERS):
        out = expand if q < 2 else reduce
        out[:, (q % 2) * PART : (q % 2 + 1) * PART] = done[y * QUARTERS + q, 0:UNITS, :]
    for row in range(TAPS * TAPS + 3):
        p, i = row // SMALL_ROWS, UNITS + row % SMALL_ROWS
        value = jnp.concatenate([done[p, i : i + 1, :], done[16 + p, i : i + 1, :]], 1)
        if row < TAPS * TAPS:
            kernel_grad[row // TAPS, row % TAPS : row % TAPS + 1, :] = value
        else:
            (gain_grad, shift_grad, scale_grad)[row - TAPS * TAPS][...] = value


def backward_kernel(grad, low, high, taps, cotangent, out, padded, shifted):
    fill_padded(padded, low, grad, high)

    def finish(r, start, chunk, value):
        upstream = cotangent[r, start : start + chunk, :].astype(F32)
        out[r, start : start + chunk, :] = (upstream + value).astype(BF16)

    def tap(a, b):
        return taps[TAPS - 1 - a, TAPS - 1 - b : TAPS - b, :]

    convolve(padded, shifted, tap, finish)


def neighbours(block):
    forward = [(i, i + 1) for i in range(QUARTERS - 1)]
    backward = [(target, source) for source, target in forward]
    low = lax.ppermute(block[ROWS - HALO :], "space", forward)
    high = lax.ppermute(block[:HALO], "space", backward)
    return low, high


def other_core(x):
    return lax.ppermute(x, "core", [(0, 1), (1, 0)])


def exchange(x, axes):
    return lax.all_to_all(x, axes, 0, 0, tiled=True)


def shards(
    pressure_tokens, dw_kernel, norm_gain, norm_shift, w_expand, w_reduce, layer_scale, cotangent
):
    tokens, upstream = pressure_tokens[0], cotangent[0]

    def copies(x):
        return jnp.broadcast_to(x[None], (DEPTH,) + x.shape)

    column = exchange(jnp.concatenate([copies(w_expand), copies(w_reduce)], 2), "z")
    column, tokens, *rows = lax.optimization_barrier(
        (column, tokens, norm_gain, norm_shift, layer_scale)
    )
    plane = column.reshape(1, BLOCK, 2 * WIDTH)
    own = exchange(jnp.broadcast_to(plane, (HEIGHT, BLOCK, 2 * WIDTH)), "y")
    low, high = neighbours(tokens)
    own, low, high, vectors = lax.optimization_barrier(
        (own.reshape(HALF, 2 * WIDTH), low, high, jnp.stack(rows))
    )
    other = other_core(own)
    padded, normed, inv_std, norm_halves, norm_t, up_halves, up_t = kernel_call(
        forward_kernel,
        [
            (PADDED, F32),
            ((CELLS, WIDTH), F32),
            ((CELLS, 1), F32),
            ((2, CELLS, PART), BF16),
            ((WIDTH, CELLS), BF16),
            ((2, CELLS, PART), BF16),
            ((WIDTH, CELLS), BF16),
        ],
        [pltpu.VMEM((CELLS, WIDTH), F32), pltpu.VMEM(SHIFTED, F32)],
        "forward",
        pl.CostEstimate(flops=8_000_000, bytes_accessed=2_000_000, transcendentals=256),
    )(tokens, low, high, dw_kernel, vectors, upstream)
    mine, theirs, block_out, mixed_grad = kernel_call(
        main_kernel,
        [
            ((PEERS, 40, 128), F32),
            ((PEERS, 40, 128), BF16),
            ((ROWS, COLS, WIDTH), BF16),
            ((ROWS, COLS, WIDTH), BF16),
        ],
        [
            pltpu.VMEM((64, WIDTH), F32),
            pltpu.VMEM((ROWS, COLS + 2 * MARGIN, WIDTH), F32),
            pltpu.VMEM((PEERS, 40, 128), F32),
        ],
        "main",
        pl.CostEstimate(flops=500_000_000, bytes_accessed=4_000_000, transcendentals=400_000),
    )(
        own, other, tokens, upstream, padded, normed, inv_std, norm_halves, norm_t, up_halves,
        up_t, vectors,
    )
    sums = (mine + other_core(theirs).astype(F32)).astype(BF16)
    sums, mixed_grad = lax.optimization_barrier((sums, mixed_grad))
    arrived = exchange(sums, ("y", "space"))
    grad_low, grad_high = neighbours(mixed_grad)
    (column,) = kernel_call(middle_kernel, [((DEPTH, 8, PART), F32)], name="middle")(arrived)
    column = exchange(column, "z")
    (grad_tokens,) = kernel_call(
        backward_kernel,
        [((ROWS, COLS, WIDTH), BF16)],
        [pltpu.VMEM(PADDED, F32), pltpu.VMEM(SHIFTED, F32)],
        "backward",
        pl.CostEstimate(flops=8_000_000, bytes_accessed=1_000_000, transcendentals=0),
    )(mixed_grad, grad_low, grad_high, dw_kernel, upstream)
    height = lax.axis_index("y").reshape(1)
    column, grad_tokens, height = lax.optimization_barrier((column, grad_tokens, height))
    (spread,) = kernel_call(spread_kernel, [((PEERS, 8, PART), F32)], name="spread")(column)
    done = exchange(spread, ("y", "space"))
    kernel_grad, gain_grad, shift_grad, scale_grad, grad_expand, grad_reduce = pl.pallas_call(
        final_kernel,
        out_shape=[
            jax.ShapeDtypeStruct(shape, F32)
            for shape in [(TAPS, TAPS, WIDTH)] + [(1, WIDTH)] * 3 + [(UNITS, WIDTH)] * 2
        ],
        in_specs=[
            pl.BlockSpec(memory_space=pltpu.SMEM),
            pl.BlockSpec(memory_space=pltpu.VMEM),
        ],
        compiler_params=pltpu.CompilerParams(vmem_limit_bytes=40 * 2**20),
        name="final",
    )(height, done)
    return (
        block_out[None],
        grad_tokens[None],
        kernel_grad,
        gain_grad[0],
        shift_grad[0],
        grad_expand,
        grad_reduce,
        scale_grad[0],
    )


def solution(mesh):
    grid = Mesh(mesh.devices.reshape(DEPTH, HEIGHT, CORES, QUARTERS), DP + ("space",))
    tokens, units = P(DP, "space", None, None), P(DP, None)
    in_specs = (tokens, P(), P(), P(), units, units, P(), tokens)
    out_specs = (tokens, tokens, P(), P(), P(), units, units, P())
    return jax.shard_map(shards, mesh=grid, in_specs=in_specs, out_specs=out_specs, check_vma=False)
```

```python
import jax
import jax.numpy as jnp
from jax import lax
from jax.experimental import pallas as pl
from jax.experimental.pallas import tpu as pltpu
from jax.sharding import Mesh, PartitionSpec as P

DEPTH, HEIGHT, CORES, QUARTERS = 16, 8, 2, 4
DP = ("z", "y", "core")
PEERS = HEIGHT * QUARTERS
ROWS, COLS, WIDTH, TAPS = 4, 64, 192, 7
CELLS = ROWS * COLS
HALO = TAPS // 2
PART = WIDTH // 2
UNITS = 3
HALF = HEIGHT * DEPTH * UNITS
BLOCK = DEPTH * UNITS
MARGIN = 8
F32, BF16 = jnp.float32, jnp.bfloat16
SMALL_ROWS = 4
PADDED = (ROWS + 2 * HALO, COLS + 2 * MARGIN, WIDTH)
SHIFTED = (TAPS, ROWS, COLS + 2 * MARGIN, WIDTH)


def kernel_call(body, outs, scratch=(), name=None, cost=None):
    return pl.pallas_call(
        body,
        out_shape=[jax.ShapeDtypeStruct(shape, kind) for shape, kind in outs],
        scratch_shapes=list(scratch),
        compiler_params=pltpu.CompilerParams(vmem_limit_bytes=40 * 2**20),
        name=name,
        cost_estimate=cost,
    )


def dot(a, b):
    return jnp.dot(a, b, preferred_element_type=F32)


def dot_rows(a, b):
    return lax.dot_general(a, b, (((0,), (0,)), ((), ())), preferred_element_type=F32)


def fill_padded(padded, low, block, high):
    padded[:, :MARGIN, :] = jnp.zeros((ROWS + 2 * HALO, MARGIN, WIDTH), F32)
    padded[:, MARGIN + COLS :, :] = jnp.zeros((ROWS + 2 * HALO, MARGIN, WIDTH), F32)
    inside = slice(MARGIN, MARGIN + COLS)
    padded[:HALO, inside, :] = low[...].astype(F32)
    padded[HALO : HALO + ROWS, inside, :] = block[...].astype(F32)
    padded[HALO + ROWS :, inside, :] = high[...].astype(F32)


def convolve(padded, shifted, tap, finish):
    for b in range(TAPS):
        taps_b = [jnp.broadcast_to(tap(a, b), (8, WIDTH)) for a in range(TAPS)]
        for t in range((MARGIN - HALO + b) // 8, (MARGIN - HALO + b + COLS + 7) // 8):
            acc = [None] * ROWS
            for i in range(ROWS + 2 * HALO):
                field = padded[i, 8 * t : 8 * t + 8, :]
                for r in range(ROWS):
                    if 0 <= i - r < TAPS:
                        term = field * taps_b[i - r]
                        acc[r] = term if acc[r] is None else acc[r] + term
            for r in range(ROWS):
                shifted[b, r, 8 * t : 8 * t + 8, :] = acc[r]
    for r in range(ROWS):
        for start in range(0, COLS, 32):
            total = None
            for b in range(TAPS):
                first = MARGIN - HALO + b + start
                value = shifted[b, r, first : first + 32, :]
                total = value if total is None else total + value
            finish(r, start, 32, total)


def forward_kernel(
    tokens, low, high, taps, vectors, cotangent,
    padded, normed, inv_std, norm_halves, norm_t, up_halves, up_t, mixed, shifted,
):
    fill_padded(padded, low, tokens, high)

    def finish(r, start, chunk, value):
        mixed[r * COLS + start : r * COLS + start + chunk, :] = value

    convolve(padded, shifted, lambda a, b: taps[a, b : b + 1, :], finish)
    value = mixed[...]
    centre = value - jnp.mean(value, -1, keepdims=True)
    inv = lax.rsqrt(jnp.mean(centre * centre, -1, keepdims=True) + 1e-06)
    norm = centre * inv
    normed[...] = norm
    inv_std[...] = inv
    rounded = (norm * vectors[0:1] + vectors[1:2]).astype(BF16)
    upstream = (cotangent[...].reshape(CELLS, WIDTH).astype(F32) * vectors[2:3]).astype(BF16)
    for h in range(2):
        norm_halves[h] = rounded[:, h * PART : (h + 1) * PART]
        up_halves[h] = upstream[:, h * PART : (h + 1) * PART]
    norm_t[...] = rounded.T
    up_t[...] = upstream.T


def main_kernel(
    own, other, tokens, cotangent, padded, normed, inv_std, norm_halves, norm_t, up_halves, up_t,
    vectors, mine, theirs_bf, block_out, mixed_grad, smalls, grad_rows, theirs,
):
    branch = jnp.zeros((CELLS, WIDTH), F32)
    normed_grad = jnp.zeros((CELLS, WIDTH), F32)
    for weights, out in ((other, theirs), (own, mine)):
        expand, reduce = weights[:, :WIDTH], weights[:, WIDTH:]
        pre = dot(expand, norm_t[...])
        hidden_grad = dot(reduce, up_t[...])
        cumulative = 0.5 * (1.0 + lax.erf(pre * 0.7071067811865476))
        hidden = (pre * cumulative).astype(BF16)
        slope = cumulative + pre * jnp.exp(-0.5 * pre * pre) * 0.3989422804014327
        pre_grad = (hidden_grad * slope).astype(BF16)
        for q in range(QUARTERS):
            left, right = (pre_grad, norm_halves) if q < 2 else (hidden, up_halves)
            grad = dot(left, right[q % 2])
            for y in range(HEIGHT):
                base = y * BLOCK
                piece = y * QUARTERS + q
                out[piece, 0:40, 0:PART] = grad[base : base + 40]
                tail = grad[base + 40 : base + 48]
                for k in range(3):
                    out[piece, 8 * k : 8 * k + 8, PART:128] = tail[:, 32 * k : 32 * k + 32]
        branch += dot_rows(hidden, reduce)
        normed_grad += dot_rows(pre_grad, expand)
    flat = tokens[...].reshape(CELLS, WIDTH).astype(F32)
    block_out[...] = (flat + vectors[2:3] * branch).astype(BF16).reshape(ROWS, COLS, WIDTH)
    norm = normed[...]
    upstream = cotangent[...].reshape(CELLS, WIDTH).astype(F32)
    smalls[TAPS * TAPS :, :] = jnp.zeros((64 - TAPS * TAPS, WIDTH), F32)
    smalls[49:50, :] = jnp.sum(normed_grad * norm, 0, keepdims=True)
    smalls[50:51, :] = jnp.sum(normed_grad, 0, keepdims=True)
    smalls[51:52, :] = jnp.sum(upstream * branch, 0, keepdims=True)
    scaled = normed_grad * vectors[0:1]
    grad = inv_std[...] * (
        scaled
        - jnp.mean(scaled, -1, keepdims=True)
        - norm * jnp.mean(scaled * norm, -1, keepdims=True)
    )
    grad_rows[:, :MARGIN, :] = jnp.zeros((ROWS, MARGIN, WIDTH), F32)
    grad_rows[:, MARGIN + COLS :, :] = jnp.zeros((ROWS, MARGIN, WIDTH), F32)
    grad_rows[:, MARGIN : MARGIN + COLS, :] = grad.reshape(ROWS, COLS, WIDTH)
    mixed_grad[...] = grad.astype(BF16).reshape(ROWS, COLS, WIDTH)
    for b in range(TAPS):
        acc = [None] * TAPS
        for t in range((MARGIN - HALO + b) // 8, (MARGIN - HALO + b + COLS + 7) // 8):
            first = 8 * t + HALO - b
            grads = [grad_rows[r, first : first + 8, :] for r in range(ROWS)]
            for i in range(ROWS + 2 * HALO):
                field = padded[i, 8 * t : 8 * t + 8, :]
                for r in range(ROWS):
                    a = i - r
                    if 0 <= a < TAPS:
                        term = field * grads[r]
                        acc[a] = term if acc[a] is None else acc[a] + term
        for a in range(TAPS):
            row = a * TAPS + b
            smalls[row : row + 1, :] = jnp.sum(acc[a], 0, keepdims=True)
    for piece in range(PEERS):
        row = SMALL_ROWS * (piece % 16)
        lane = PART * (piece // 16)
        values = smalls[row : row + SMALL_ROWS, lane : lane + PART]
        for out in (mine, theirs):
            for k in range(3):
                at = 24 + SMALL_ROWS * k
                out[piece, at : at + SMALL_ROWS, PART:128] = values[:, 32 * k : 32 * k + 32]
            out[piece, 36:40, PART:128] = jnp.zeros((4, 32), F32)
    theirs_bf[...] = theirs[...].astype(BF16)


def middle_kernel(arrived, column):
    total = arrived[0].astype(F32)
    for p in range(1, PEERS):
        total += arrived[p].astype(F32)
    tail = jnp.concatenate([total[8 * k : 8 * k + 8, PART:128] for k in range(3)], 1)
    grad = jnp.concatenate([total[:, :PART], tail], 0)
    at = [24 + SMALL_ROWS * k for k in range(3)]
    small = jnp.concatenate([total[i : i + SMALL_ROWS, PART:128] for i in at], 1)
    blank = jnp.zeros((1, PART), F32)
    for z in range(DEPTH):
        rows = [grad[z * UNITS : (z + 1) * UNITS], small, blank]
        column[z] = jnp.concatenate(rows, 0).astype(BF16)


def spread_kernel(arrived, copies):
    total = jnp.sum(arrived[...].astype(F32), 0).astype(BF16)
    for p in range(PEERS):
        copies[p] = total


def final_kernel(height, done, kernel_grad, gain_grad, shift_grad, scale_grad, expand, reduce):
    y = height[0]
    for q in range(QUARTERS):
        out = expand if q < 2 else reduce
        block = done[y * QUARTERS + q].astype(F32)
        out[:, (q % 2) * PART : (q % 2 + 1) * PART] = block[0:UNITS]
    for p in range((TAPS * TAPS + 3 + SMALL_ROWS - 1) // SMALL_ROWS):
        block = jnp.concatenate([done[p].astype(F32), done[16 + p].astype(F32)], 1)
        for i in range(SMALL_ROWS):
            row = SMALL_ROWS * p + i
            value = block[UNITS + i : UNITS + i + 1]
            if row < TAPS * TAPS:
                kernel_grad[row // TAPS, row % TAPS : row % TAPS + 1, :] = value
            else:
                (gain_grad, shift_grad, scale_grad)[row - TAPS * TAPS][...] = value


def backward_kernel(grad, low, high, taps, cotangent, out, padded, shifted):
    fill_padded(padded, low, grad, high)

    def finish(r, start, chunk, value):
        upstream = cotangent[r, start : start + chunk, :].astype(F32)
        out[r, start : start + chunk, :] = (upstream + value).astype(BF16)

    def tap(a, b):
        return taps[TAPS - 1 - a, TAPS - 1 - b : TAPS - b, :]

    convolve(padded, shifted, tap, finish)


def neighbours(block):
    forward = [(i, i + 1) for i in range(QUARTERS - 1)]
    backward = [(target, source) for source, target in forward]
    low = lax.ppermute(block[ROWS - HALO :], "space", forward)
    high = lax.ppermute(block[:HALO], "space", backward)
    return low, high


def other_core(x):
    return lax.ppermute(x, "core", [(0, 1), (1, 0)])


def exchange(x, axes):
    return lax.all_to_all(x, axes, 0, 0, tiled=True)


def shards(
    pressure_tokens, dw_kernel, norm_gain, norm_shift, w_expand, w_reduce, layer_scale, cotangent
):
    tokens, upstream = pressure_tokens[0], cotangent[0]

    def copies(x):
        return jnp.broadcast_to(x[None], (DEPTH,) + x.shape)

    column = exchange(jnp.concatenate([copies(w_expand), copies(w_reduce)], 2), "z")
    low, high = neighbours(tokens)
    vectors = jnp.stack([norm_gain, norm_shift, layer_scale])
    column, low, high, vectors = lax.optimization_barrier((column, low, high, vectors))
    plane = column.reshape(1, BLOCK, 2 * WIDTH)
    own = exchange(jnp.broadcast_to(plane, (HEIGHT, BLOCK, 2 * WIDTH)), "y")
    own, low = lax.optimization_barrier((own.reshape(HALF, 2 * WIDTH), low))
    other = other_core(own)
    padded, normed, inv_std, norm_halves, norm_t, up_halves, up_t = kernel_call(
        forward_kernel,
        [
            (PADDED, F32),
            ((CELLS, WIDTH), F32),
            ((CELLS, 1), F32),
            ((2, CELLS, PART), BF16),
            ((WIDTH, CELLS), BF16),
            ((2, CELLS, PART), BF16),
            ((WIDTH, CELLS), BF16),
        ],
        [pltpu.VMEM((CELLS, WIDTH), F32), pltpu.VMEM(SHIFTED, F32)],
        "forward",
        pl.CostEstimate(flops=8_000_000, bytes_accessed=2_000_000, transcendentals=256),
    )(tokens, low, high, dw_kernel, vectors, upstream)
    mine, theirs, block_out, mixed_grad = kernel_call(
        main_kernel,
        [
            ((PEERS, 40, 128), F32),
            ((PEERS, 40, 128), BF16),
            ((ROWS, COLS, WIDTH), BF16),
            ((ROWS, COLS, WIDTH), BF16),
        ],
        [
            pltpu.VMEM((64, WIDTH), F32),
            pltpu.VMEM((ROWS, COLS + 2 * MARGIN, WIDTH), F32),
            pltpu.VMEM((PEERS, 40, 128), F32),
        ],
        "main",
        pl.CostEstimate(flops=500_000_000, bytes_accessed=4_000_000, transcendentals=400_000),
    )(
        own, other, tokens, upstream, padded, normed, inv_std, norm_halves, norm_t, up_halves,
        up_t, vectors,
    )
    sums = (mine + other_core(theirs).astype(F32)).astype(BF16)
    sums, mixed_grad = lax.optimization_barrier((sums, mixed_grad))
    arrived = exchange(sums, ("y", "space"))
    grad_low, grad_high = neighbours(mixed_grad)
    (column,) = kernel_call(middle_kernel, [((DEPTH, 8, PART), BF16)], name="middle")(arrived)
    column = exchange(column, "z")
    (grad_tokens,) = kernel_call(
        backward_kernel,
        [((ROWS, COLS, WIDTH), BF16)],
        [pltpu.VMEM(PADDED, F32), pltpu.VMEM(SHIFTED, F32)],
        "backward",
        pl.CostEstimate(flops=8_000_000, bytes_accessed=1_000_000, transcendentals=0),
    )(mixed_grad, grad_low, grad_high, dw_kernel, upstream)
    height = lax.axis_index("y").reshape(1)
    column, grad_tokens, height = lax.optimization_barrier((column, grad_tokens, height))
    (spread,) = kernel_call(spread_kernel, [((PEERS, 8, PART), BF16)], name="spread")(column)
    done = exchange(spread, ("y", "space"))
    kernel_grad, gain_grad, shift_grad, scale_grad, grad_expand, grad_reduce = pl.pallas_call(
        final_kernel,
        out_shape=[
            jax.ShapeDtypeStruct(shape, F32)
            for shape in [(TAPS, TAPS, WIDTH)] + [(1, WIDTH)] * 3 + [(UNITS, WIDTH)] * 2
        ],
        in_specs=[
            pl.BlockSpec(memory_space=pltpu.SMEM),
            pl.BlockSpec(memory_space=pltpu.VMEM),
        ],
        compiler_params=pltpu.CompilerParams(vmem_limit_bytes=40 * 2**20),
        name="final",
    )(height, done)
    return (
        block_out[None],
        grad_tokens[None],
        kernel_grad,
        gain_grad[0],
        shift_grad[0],
        grad_expand,
        grad_reduce,
        scale_grad[0],
    )


def solution(mesh):
    grid = Mesh(mesh.devices.reshape(DEPTH, HEIGHT, CORES, QUARTERS), DP + ("space",))
    tokens, units = P(DP, "space", None, None), P(DP, None)
    in_specs = (tokens, P(), P(), P(), units, units, P(), tokens)
    out_specs = (tokens, tokens, P(), P(), P(), units, units, P())
    return jax.shard_map(shards, mesh=grid, in_specs=in_specs, out_specs=out_specs, check_vma=False)
```

```python
import jax
import jax.numpy as jnp
from jax import lax
from jax.experimental import pallas as pl
from jax.experimental.pallas import tpu as pltpu
from jax.sharding import Mesh, PartitionSpec as P

DEPTH, HEIGHT, CORES, QUARTERS = 16, 8, 2, 4
DP = ("z", "y", "core")
PEERS = HEIGHT * QUARTERS
ROWS, COLS, WIDTH, TAPS = 4, 64, 192, 7
CELLS = ROWS * COLS
HALO = TAPS // 2
PART = WIDTH // 2
UNITS = 3
HALF = HEIGHT * DEPTH * UNITS
BLOCK = DEPTH * UNITS
MARGIN = 8
F32, BF16 = jnp.float32, jnp.bfloat16
SMALL_ROWS = 4
FIRST_Z, FIRST_Y, FIRST_X = 12, 4, 2
PADDED = (ROWS + 2 * HALO, COLS + 2 * MARGIN, WIDTH)
SHIFTED = (TAPS, ROWS, COLS + 2 * MARGIN, WIDTH)


def kernel_call(body, outs, scratch=(), name=None, cost=None):
    return pl.pallas_call(
        body,
        out_shape=[jax.ShapeDtypeStruct(shape, kind) for shape, kind in outs],
        scratch_shapes=list(scratch),
        compiler_params=pltpu.CompilerParams(vmem_limit_bytes=40 * 2**20),
        name=name,
        cost_estimate=cost,
    )


def dot(a, b):
    return jnp.dot(a, b, preferred_element_type=F32)


def dot_rows(a, b):
    return lax.dot_general(a, b, (((0,), (0,)), ((), ())), preferred_element_type=F32)


def fill_padded(padded, low, block, high):
    padded[:, :MARGIN, :] = jnp.zeros((ROWS + 2 * HALO, MARGIN, WIDTH), F32)
    padded[:, MARGIN + COLS :, :] = jnp.zeros((ROWS + 2 * HALO, MARGIN, WIDTH), F32)
    inside = slice(MARGIN, MARGIN + COLS)
    padded[:HALO, inside, :] = low[...].astype(F32)
    padded[HALO : HALO + ROWS, inside, :] = block[...].astype(F32)
    padded[HALO + ROWS :, inside, :] = high[...].astype(F32)


def convolve(padded, shifted, tap, finish):
    for b in range(TAPS):
        taps_b = [jnp.broadcast_to(tap(a, b), (8, WIDTH)) for a in range(TAPS)]
        for t in range((MARGIN - HALO + b) // 8, (MARGIN - HALO + b + COLS + 7) // 8):
            acc = [None] * ROWS
            for i in range(ROWS + 2 * HALO):
                field = padded[i, 8 * t : 8 * t + 8, :]
                for r in range(ROWS):
                    if 0 <= i - r < TAPS:
                        term = field * taps_b[i - r]
                        acc[r] = term if acc[r] is None else acc[r] + term
            for r in range(ROWS):
                shifted[b, r, 8 * t : 8 * t + 8, :] = acc[r]
    for r in range(ROWS):
        for start in range(0, COLS, 32):
            total = None
            for b in range(TAPS):
                first = MARGIN - HALO + b + start
                value = shifted[b, r, first : first + 32, :]
                total = value if total is None else total + value
            finish(r, start, 32, total)


def forward_kernel(
    tokens, low, high, taps, vectors, cotangent,
    padded, normed, inv_std, norm_halves, norm_t, up_halves, up_t, mixed, shifted,
):
    fill_padded(padded, low, tokens, high)

    def finish(r, start, chunk, value):
        mixed[r * COLS + start : r * COLS + start + chunk, :] = value

    convolve(padded, shifted, lambda a, b: taps[a, b : b + 1, :], finish)
    value = mixed[...]
    centre = value - jnp.mean(value, -1, keepdims=True)
    inv = lax.rsqrt(jnp.mean(centre * centre, -1, keepdims=True) + 1e-06)
    norm = centre * inv
    normed[...] = norm
    inv_std[...] = inv
    rounded = (norm * vectors[0:1] + vectors[1:2]).astype(BF16)
    upstream = (cotangent[...].reshape(CELLS, WIDTH).astype(F32) * vectors[2:3]).astype(BF16)
    for h in range(2):
        norm_halves[h] = rounded[:, h * PART : (h + 1) * PART]
        up_halves[h] = upstream[:, h * PART : (h + 1) * PART]
    norm_t[...] = rounded.T
    up_t[...] = upstream.T


def main_kernel(
    own, other, tokens, cotangent, padded, normed, inv_std, norm_halves, norm_t, up_halves, up_t,
    vectors, mine, theirs_bf, block_out, mixed_grad, smalls, grad_rows, theirs,
):
    branch = jnp.zeros((CELLS, WIDTH), F32)
    normed_grad = jnp.zeros((CELLS, WIDTH), F32)
    for weights, out in ((other, theirs), (own, mine)):
        expand, reduce = weights[:, :WIDTH], weights[:, WIDTH:]
        pre = dot(expand, norm_t[...])
        hidden_grad = dot(reduce, up_t[...])
        cumulative = 0.5 * (1.0 + lax.erf(pre * 0.7071067811865476))
        hidden = (pre * cumulative).astype(BF16)
        slope = cumulative + pre * jnp.exp(-0.5 * pre * pre) * 0.3989422804014327
        pre_grad = (hidden_grad * slope).astype(BF16)
        for q in range(QUARTERS):
            left, right = (pre_grad, norm_halves) if q < 2 else (hidden, up_halves)
            grad = dot(left, right[q % 2])
            for y in range(HEIGHT):
                base = y * BLOCK
                piece = y * QUARTERS + q
                out[piece, 0:40, 0:PART] = grad[base : base + 40]
                tail = grad[base + 40 : base + 48]
                for k in range(3):
                    out[piece, 8 * k : 8 * k + 8, PART:128] = tail[:, 32 * k : 32 * k + 32]
        branch += dot_rows(hidden, reduce)
        normed_grad += dot_rows(pre_grad, expand)
    flat = tokens[...].reshape(CELLS, WIDTH).astype(F32)
    block_out[...] = (flat + vectors[2:3] * branch).astype(BF16).reshape(ROWS, COLS, WIDTH)
    norm = normed[...]
    upstream = cotangent[...].reshape(CELLS, WIDTH).astype(F32)
    smalls[TAPS * TAPS :, :] = jnp.zeros((64 - TAPS * TAPS, WIDTH), F32)
    smalls[49:50, :] = jnp.sum(normed_grad * norm, 0, keepdims=True)
    smalls[50:51, :] = jnp.sum(normed_grad, 0, keepdims=True)
    smalls[51:52, :] = jnp.sum(upstream * branch, 0, keepdims=True)
    scaled = normed_grad * vectors[0:1]
    grad = inv_std[...] * (
        scaled
        - jnp.mean(scaled, -1, keepdims=True)
        - norm * jnp.mean(scaled * norm, -1, keepdims=True)
    )
    grad_rows[:, :MARGIN, :] = jnp.zeros((ROWS, MARGIN, WIDTH), F32)
    grad_rows[:, MARGIN + COLS :, :] = jnp.zeros((ROWS, MARGIN, WIDTH), F32)
    grad_rows[:, MARGIN : MARGIN + COLS, :] = grad.reshape(ROWS, COLS, WIDTH)
    mixed_grad[...] = grad.astype(BF16).reshape(ROWS, COLS, WIDTH)
    for b in range(TAPS):
        acc = [None] * TAPS
        for t in range((MARGIN - HALO + b) // 8, (MARGIN - HALO + b + COLS + 7) // 8):
            first = 8 * t + HALO - b
            grads = [grad_rows[r, first : first + 8, :] for r in range(ROWS)]
            for i in range(ROWS + 2 * HALO):
                field = padded[i, 8 * t : 8 * t + 8, :]
                for r in range(ROWS):
                    a = i - r
                    if 0 <= a < TAPS:
                        term = field * grads[r]
                        acc[a] = term if acc[a] is None else acc[a] + term
        for a in range(TAPS):
            row = a * TAPS + b
            smalls[row : row + 1, :] = jnp.sum(acc[a], 0, keepdims=True)
    for piece in range(PEERS):
        row = SMALL_ROWS * (piece % 16)
        lane = PART * (piece // 16)
        values = smalls[row : row + SMALL_ROWS, lane : lane + PART]
        for out in (mine, theirs):
            for k in range(3):
                at = 24 + SMALL_ROWS * k
                out[piece, at : at + SMALL_ROWS, PART:128] = values[:, 32 * k : 32 * k + 32]
            out[piece, 36:40, PART:128] = jnp.zeros((4, 32), F32)
    theirs_bf[...] = theirs[...].astype(BF16)


def middle_kernel(arrived, column):
    total = arrived[0].astype(F32)
    for p in range(1, PEERS):
        total += arrived[p].astype(F32)
    tail = jnp.concatenate([total[8 * k : 8 * k + 8, PART:128] for k in range(3)], 1)
    grad = jnp.concatenate([total[:, :PART], tail], 0)
    at = [24 + SMALL_ROWS * k for k in range(3)]
    small = jnp.concatenate([total[i : i + SMALL_ROWS, PART:128] for i in at], 1)
    blank = jnp.zeros((1, PART), F32)
    for z in range(DEPTH):
        rows = [grad[z * UNITS : (z + 1) * UNITS], small, blank]
        column[z] = jnp.concatenate(rows, 0).astype(BF16)


def spread_kernel(arrived, copies):
    total = jnp.sum(arrived[...].astype(F32), 0).astype(BF16)
    for p in range(PEERS):
        copies[p] = total


def final_kernel(height, done, kernel_grad, gain_grad, shift_grad, scale_grad, expand, reduce):
    y = height[0]
    for q in range(QUARTERS):
        out = expand if q < 2 else reduce
        block = done[y * QUARTERS + q].astype(F32)
        out[:, (q % 2) * PART : (q % 2 + 1) * PART] = block[0:UNITS]
    for p in range((TAPS * TAPS + 3 + SMALL_ROWS - 1) // SMALL_ROWS):
        block = jnp.concatenate([done[p].astype(F32), done[16 + p].astype(F32)], 1)
        for i in range(SMALL_ROWS):
            row = SMALL_ROWS * p + i
            value = block[UNITS + i : UNITS + i + 1]
            if row < TAPS * TAPS:
                kernel_grad[row // TAPS, row % TAPS : row % TAPS + 1, :] = value
            else:
                (gain_grad, shift_grad, scale_grad)[row - TAPS * TAPS][...] = value


def backward_kernel(grad, low, high, taps, cotangent, out, padded, shifted):
    fill_padded(padded, low, grad, high)

    def finish(r, start, chunk, value):
        upstream = cotangent[r, start : start + chunk, :].astype(F32)
        out[r, start : start + chunk, :] = (upstream + value).astype(BF16)

    def tap(a, b):
        return taps[TAPS - 1 - a, TAPS - 1 - b : TAPS - b, :]

    convolve(padded, shifted, tap, finish)


def neighbours(block):
    forward = [(i, i + 1) for i in range(QUARTERS - 1)]
    backward = [(target, source) for source, target in forward]
    low = lax.ppermute(block[ROWS - HALO :], "space", forward)
    high = lax.ppermute(block[:HALO], "space", backward)
    return low, high


def other_core(x):
    return lax.ppermute(x, "core", [(0, 1), (1, 0)])


def turned(count, first):
    return [(i + first) % count for i in range(count)]


ORDERS = {
    "z": turned(DEPTH, FIRST_Z),
    "y": turned(HEIGHT, FIRST_Y),
    ("y", "space"): [
        y * QUARTERS + x for y in turned(HEIGHT, FIRST_Y) for x in turned(QUARTERS, FIRST_X)
    ],
}


def exchange(x, axes):
    return lax.all_to_all(x, axes, 0, 0, axis_index_groups=[ORDERS[axes]], tiled=True)


def shards(
    pressure_tokens, dw_kernel, norm_gain, norm_shift, w_expand, w_reduce, layer_scale, cotangent
):
    tokens, upstream = pressure_tokens[0], cotangent[0]

    def copies(x):
        return jnp.broadcast_to(x[None], (DEPTH,) + x.shape)

    column = exchange(jnp.concatenate([copies(w_expand), copies(w_reduce)], 2), "z")
    column, tokens, *rows = lax.optimization_barrier(
        (column, tokens, norm_gain, norm_shift, layer_scale)
    )
    plane = column.reshape(1, BLOCK, 2 * WIDTH)
    own = exchange(jnp.broadcast_to(plane, (HEIGHT, BLOCK, 2 * WIDTH)), "y")
    low, high = neighbours(tokens)
    own, low, high, vectors = lax.optimization_barrier(
        (own.reshape(HALF, 2 * WIDTH), low, high, jnp.stack(rows))
    )
    other = other_core(own)
    padded, normed, inv_std, norm_halves, norm_t, up_halves, up_t = kernel_call(
        forward_kernel,
        [
            (PADDED, F32),
            ((CELLS, WIDTH), F32),
            ((CELLS, 1), F32),
            ((2, CELLS, PART), BF16),
            ((WIDTH, CELLS), BF16),
            ((2, CELLS, PART), BF16),
            ((WIDTH, CELLS), BF16),
        ],
        [pltpu.VMEM((CELLS, WIDTH), F32), pltpu.VMEM(SHIFTED, F32)],
        "forward",
        pl.CostEstimate(flops=8_000_000, bytes_accessed=2_000_000, transcendentals=256),
    )(tokens, low, high, dw_kernel, vectors, upstream)
    mine, theirs, block_out, mixed_grad = kernel_call(
        main_kernel,
        [
            ((PEERS, 40, 128), F32),
            ((PEERS, 40, 128), BF16),
            ((ROWS, COLS, WIDTH), BF16),
            ((ROWS, COLS, WIDTH), BF16),
        ],
        [
            pltpu.VMEM((64, WIDTH), F32),
            pltpu.VMEM((ROWS, COLS + 2 * MARGIN, WIDTH), F32),
            pltpu.VMEM((PEERS, 40, 128), F32),
        ],
        "main",
        pl.CostEstimate(flops=500_000_000, bytes_accessed=4_000_000, transcendentals=400_000),
    )(
        own, other, tokens, upstream, padded, normed, inv_std, norm_halves, norm_t, up_halves,
        up_t, vectors,
    )
    sums = (mine + other_core(theirs).astype(F32)).astype(BF16)
    sums, mixed_grad = lax.optimization_barrier((sums, mixed_grad))
    arrived = exchange(sums, ("y", "space"))
    grad_low, grad_high = neighbours(mixed_grad)
    arrived, grad_low, grad_high = lax.optimization_barrier((arrived, grad_low, grad_high))
    (column,) = kernel_call(middle_kernel, [((DEPTH, 8, PART), BF16)], name="middle")(arrived)
    column = exchange(column, "z")
    (grad_tokens,) = kernel_call(
        backward_kernel,
        [((ROWS, COLS, WIDTH), BF16)],
        [pltpu.VMEM(PADDED, F32), pltpu.VMEM(SHIFTED, F32)],
        "backward",
        pl.CostEstimate(flops=8_000_000, bytes_accessed=1_000_000, transcendentals=0),
    )(mixed_grad, grad_low, grad_high, dw_kernel, upstream)
    height = lax.rem(lax.axis_index("y") + (HEIGHT - FIRST_Y), HEIGHT).reshape(1)
    column, grad_tokens, height = lax.optimization_barrier((column, grad_tokens, height))
    (spread,) = kernel_call(spread_kernel, [((PEERS, 8, PART), BF16)], name="spread")(column)
    done = exchange(spread, ("y", "space"))
    kernel_grad, gain_grad, shift_grad, scale_grad, grad_expand, grad_reduce = pl.pallas_call(
        final_kernel,
        out_shape=[
            jax.ShapeDtypeStruct(shape, F32)
            for shape in [(TAPS, TAPS, WIDTH)] + [(1, WIDTH)] * 3 + [(UNITS, WIDTH)] * 2
        ],
        in_specs=[
            pl.BlockSpec(memory_space=pltpu.SMEM),
            pl.BlockSpec(memory_space=pltpu.VMEM),
        ],
        compiler_params=pltpu.CompilerParams(vmem_limit_bytes=40 * 2**20),
        name="final",
    )(height, done)
    return (
        block_out[None],
        grad_tokens[None],
        kernel_grad,
        gain_grad[0],
        shift_grad[0],
        grad_expand,
        grad_reduce,
        scale_grad[0],
    )


def solution(mesh):
    grid = Mesh(mesh.devices.reshape(DEPTH, HEIGHT, CORES, QUARTERS), DP + ("space",))
    tokens, units = P(DP, "space", None, None), P(DP, None)
    in_specs = (tokens, P(), P(), P(), units, units, P(), tokens)
    out_specs = (tokens, tokens, P(), P(), P(), units, units, P())
    return jax.shard_map(shards, mesh=grid, in_specs=in_specs, out_specs=out_specs, check_vma=False)
```

```python
import jax
import jax.numpy as jnp
from jax import lax
from jax.experimental import pallas as pl
from jax.experimental.pallas import tpu as pltpu
from jax.sharding import Mesh, PartitionSpec as P

DEPTH, HEIGHT, CORES, QUARTERS = 16, 8, 2, 4
DP = ("z", "y", "core")
PEERS = HEIGHT * QUARTERS
ROWS, COLS, WIDTH, TAPS = 4, 64, 192, 7
CELLS = ROWS * COLS
HALO = TAPS // 2
PART = WIDTH // 2
UNITS = 3
HALF = HEIGHT * DEPTH * UNITS
BLOCK = DEPTH * UNITS
MARGIN = 8
F32, BF16 = jnp.float32, jnp.bfloat16
SMALL_ROWS = 4
FIRST_Z, LAST_Z, FIRST_Y, FIRST_X = 14, 8, 4, 2
PADDED = (ROWS + 2 * HALO, COLS + 2 * MARGIN, WIDTH)
SHIFTED = (TAPS, ROWS, COLS + 2 * MARGIN, WIDTH)


def kernel_call(body, outs, scratch=(), name=None, cost=None):
    return pl.pallas_call(
        body,
        out_shape=[jax.ShapeDtypeStruct(shape, kind) for shape, kind in outs],
        scratch_shapes=list(scratch),
        compiler_params=pltpu.CompilerParams(vmem_limit_bytes=40 * 2**20),
        name=name,
        cost_estimate=cost,
    )


def dot(a, b):
    return jnp.dot(a, b, preferred_element_type=F32)


def dot_rows(a, b):
    return lax.dot_general(a, b, (((0,), (0,)), ((), ())), preferred_element_type=F32)


def fill_padded(padded, low, block, high):
    padded[:, :MARGIN, :] = jnp.zeros((ROWS + 2 * HALO, MARGIN, WIDTH), F32)
    padded[:, MARGIN + COLS :, :] = jnp.zeros((ROWS + 2 * HALO, MARGIN, WIDTH), F32)
    inside = slice(MARGIN, MARGIN + COLS)
    padded[:HALO, inside, :] = low[...].astype(F32)
    padded[HALO : HALO + ROWS, inside, :] = block[...].astype(F32)
    padded[HALO + ROWS :, inside, :] = high[...].astype(F32)


def convolve(padded, shifted, tap, finish):
    for b in range(TAPS):
        taps_b = [jnp.broadcast_to(tap(a, b), (8, WIDTH)) for a in range(TAPS)]
        for t in range((MARGIN - HALO + b) // 8, (MARGIN - HALO + b + COLS + 7) // 8):
            acc = [None] * ROWS
            for i in range(ROWS + 2 * HALO):
                field = padded[i, 8 * t : 8 * t + 8, :]
                for r in range(ROWS):
                    if 0 <= i - r < TAPS:
                        term = field * taps_b[i - r]
                        acc[r] = term if acc[r] is None else acc[r] + term
            for r in range(ROWS):
                shifted[b, r, 8 * t : 8 * t + 8, :] = acc[r]
    for r in range(ROWS):
        for start in range(0, COLS, 32):
            total = None
            for b in range(TAPS):
                first = MARGIN - HALO + b + start
                value = shifted[b, r, first : first + 32, :]
                total = value if total is None else total + value
            finish(r, start, 32, total)


def forward_kernel(
    tokens, low, high, taps, vectors, cotangent,
    padded, normed, inv_std, norm_halves, norm_t, up_halves, up_t, mixed, shifted,
):
    fill_padded(padded, low, tokens, high)

    def finish(r, start, chunk, value):
        mixed[r * COLS + start : r * COLS + start + chunk, :] = value

    convolve(padded, shifted, lambda a, b: taps[a, b : b + 1, :], finish)
    value = mixed[...]
    centre = value - jnp.mean(value, -1, keepdims=True)
    inv = lax.rsqrt(jnp.mean(centre * centre, -1, keepdims=True) + 1e-06)
    norm = centre * inv
    normed[...] = norm
    inv_std[...] = inv
    rounded = (norm * vectors[0:1] + vectors[1:2]).astype(BF16)
    upstream = (cotangent[...].reshape(CELLS, WIDTH).astype(F32) * vectors[2:3]).astype(BF16)
    for h in range(2):
        norm_halves[h] = rounded[:, h * PART : (h + 1) * PART]
        up_halves[h] = upstream[:, h * PART : (h + 1) * PART]
    norm_t[...] = rounded.T
    up_t[...] = upstream.T


def main_kernel(
    own, other, tokens, cotangent, padded, normed, inv_std, norm_halves, norm_t, up_halves, up_t,
    vectors, mine, theirs_bf, block_out, mixed_grad, smalls, grad_rows, theirs,
):
    branch = jnp.zeros((CELLS, WIDTH), F32)
    normed_grad = jnp.zeros((CELLS, WIDTH), F32)
    for weights, out in ((other, theirs), (own, mine)):
        expand, reduce = weights[:, :WIDTH], weights[:, WIDTH:]
        pre = dot(expand, norm_t[...])
        hidden_grad = dot(reduce, up_t[...])
        cumulative = 0.5 * (1.0 + lax.erf(pre * 0.7071067811865476))
        hidden = (pre * cumulative).astype(BF16)
        slope = cumulative + pre * jnp.exp(-0.5 * pre * pre) * 0.3989422804014327
        pre_grad = (hidden_grad * slope).astype(BF16)
        for q in range(QUARTERS):
            left, right = (pre_grad, norm_halves) if q < 2 else (hidden, up_halves)
            grad = dot(left, right[q % 2])
            for y in range(HEIGHT):
                base = y * BLOCK
                piece = y * QUARTERS + q
                out[piece, 0:40, 0:PART] = grad[base : base + 40]
                tail = grad[base + 40 : base + 48]
                for k in range(3):
                    out[piece, 8 * k : 8 * k + 8, PART:128] = tail[:, 32 * k : 32 * k + 32]
        branch += dot_rows(hidden, reduce)
        normed_grad += dot_rows(pre_grad, expand)
    flat = tokens[...].reshape(CELLS, WIDTH).astype(F32)
    block_out[...] = (flat + vectors[2:3] * branch).astype(BF16).reshape(ROWS, COLS, WIDTH)
    norm = normed[...]
    upstream = cotangent[...].reshape(CELLS, WIDTH).astype(F32)
    smalls[TAPS * TAPS :, :] = jnp.zeros((64 - TAPS * TAPS, WIDTH), F32)
    smalls[49:50, :] = jnp.sum(normed_grad * norm, 0, keepdims=True)
    smalls[50:51, :] = jnp.sum(normed_grad, 0, keepdims=True)
    smalls[51:52, :] = jnp.sum(upstream * branch, 0, keepdims=True)
    scaled = normed_grad * vectors[0:1]
    grad = inv_std[...] * (
        scaled
        - jnp.mean(scaled, -1, keepdims=True)
        - norm * jnp.mean(scaled * norm, -1, keepdims=True)
    )
    grad_rows[:, :MARGIN, :] = jnp.zeros((ROWS, MARGIN, WIDTH), F32)
    grad_rows[:, MARGIN + COLS :, :] = jnp.zeros((ROWS, MARGIN, WIDTH), F32)
    grad_rows[:, MARGIN : MARGIN + COLS, :] = grad.reshape(ROWS, COLS, WIDTH)
    mixed_grad[...] = grad.astype(BF16).reshape(ROWS, COLS, WIDTH)
    for b in range(TAPS):
        acc = [None] * TAPS
        for t in range((MARGIN - HALO + b) // 8, (MARGIN - HALO + b + COLS + 7) // 8):
            first = 8 * t + HALO - b
            grads = [grad_rows[r, first : first + 8, :] for r in range(ROWS)]
            for i in range(ROWS + 2 * HALO):
                field = padded[i, 8 * t : 8 * t + 8, :]
                for r in range(ROWS):
                    a = i - r
                    if 0 <= a < TAPS:
                        term = field * grads[r]
                        acc[a] = term if acc[a] is None else acc[a] + term
        for a in range(TAPS):
            row = a * TAPS + b
            smalls[row : row + 1, :] = jnp.sum(acc[a], 0, keepdims=True)
    for piece in range(PEERS):
        row = SMALL_ROWS * (piece % 16)
        lane = PART * (piece // 16)
        values = smalls[row : row + SMALL_ROWS, lane : lane + PART]
        for out in (mine, theirs):
            for k in range(3):
                at = 24 + SMALL_ROWS * k
                out[piece, at : at + SMALL_ROWS, PART:128] = values[:, 32 * k : 32 * k + 32]
            out[piece, 36:40, PART:128] = jnp.zeros((4, 32), F32)
    theirs_bf[...] = theirs[...].astype(BF16)


def middle_kernel(arrived, column):
    total = arrived[0].astype(F32)
    for p in range(1, PEERS):
        total += arrived[p].astype(F32)
    tail = jnp.concatenate([total[8 * k : 8 * k + 8, PART:128] for k in range(3)], 1)
    grad = jnp.concatenate([total[:, :PART], tail], 0)
    at = [24 + SMALL_ROWS * k for k in range(3)]
    small = jnp.concatenate([total[i : i + SMALL_ROWS, PART:128] for i in at], 1)
    blank = jnp.zeros((1, PART), F32)
    for z in range(DEPTH):
        rows = [grad[z * UNITS : (z + 1) * UNITS], small, blank]
        column[(z + FIRST_Z - LAST_Z) % DEPTH] = jnp.concatenate(rows, 0).astype(BF16)


def spread_kernel(arrived, copies):
    total = jnp.sum(arrived[...].astype(F32), 0).astype(BF16)
    for p in range(PEERS):
        copies[p] = total


def final_kernel(height, done, kernel_grad, gain_grad, shift_grad, scale_grad, expand, reduce):
    y = height[0]
    for q in range(QUARTERS):
        out = expand if q < 2 else reduce
        block = done[y * QUARTERS + q].astype(F32)
        out[:, (q % 2) * PART : (q % 2 + 1) * PART] = block[0:UNITS]
    for p in range((TAPS * TAPS + 3 + SMALL_ROWS - 1) // SMALL_ROWS):
        block = jnp.concatenate([done[p].astype(F32), done[16 + p].astype(F32)], 1)
        for i in range(SMALL_ROWS):
            row = SMALL_ROWS * p + i
            value = block[UNITS + i : UNITS + i + 1]
            if row < TAPS * TAPS:
                kernel_grad[row // TAPS, row % TAPS : row % TAPS + 1, :] = value
            else:
                (gain_grad, shift_grad, scale_grad)[row - TAPS * TAPS][...] = value


def backward_kernel(grad, low, high, taps, cotangent, out, padded, shifted):
    fill_padded(padded, low, grad, high)

    def finish(r, start, chunk, value):
        upstream = cotangent[r, start : start + chunk, :].astype(F32)
        out[r, start : start + chunk, :] = (upstream + value).astype(BF16)

    def tap(a, b):
        return taps[TAPS - 1 - a, TAPS - 1 - b : TAPS - b, :]

    convolve(padded, shifted, tap, finish)


def neighbours(block):
    forward = [(i, i + 1) for i in range(QUARTERS - 1)]
    backward = [(target, source) for source, target in forward]
    low = lax.ppermute(block[ROWS - HALO :], "space", forward)
    high = lax.ppermute(block[:HALO], "space", backward)
    return low, high


def other_core(x):
    return lax.ppermute(x, "core", [(0, 1), (1, 0)])


def turned(count, first):
    return [(i + first) % count for i in range(count)]


ORDERS = {
    "z": turned(DEPTH, FIRST_Z),
    "z_back": turned(DEPTH, LAST_Z),
    "y": turned(HEIGHT, FIRST_Y),
    ("y", "space"): [
        y * QUARTERS + x for y in turned(HEIGHT, FIRST_Y) for x in turned(QUARTERS, FIRST_X)
    ],
}


def exchange(x, axes, order=None):
    groups = [ORDERS[order or axes]]
    return lax.all_to_all(x, axes, 0, 0, axis_index_groups=groups, tiled=True)


def shards(
    pressure_tokens, dw_kernel, norm_gain, norm_shift, w_expand, w_reduce, layer_scale, cotangent
):
    tokens, upstream = pressure_tokens[0], cotangent[0]

    def copies(x):
        return jnp.broadcast_to(x[None], (DEPTH,) + x.shape)

    column = exchange(jnp.concatenate([copies(w_expand), copies(w_reduce)], 2), "z")
    low, high = neighbours(tokens)
    vectors = jnp.stack([norm_gain, norm_shift, layer_scale])
    column, low, high, vectors = lax.optimization_barrier((column, low, high, vectors))
    plane = column.reshape(1, BLOCK, 2 * WIDTH)
    own = exchange(jnp.broadcast_to(plane, (HEIGHT, BLOCK, 2 * WIDTH)), "y")
    own, low = lax.optimization_barrier((own.reshape(HALF, 2 * WIDTH), low))
    other = other_core(own)
    padded, normed, inv_std, norm_halves, norm_t, up_halves, up_t = kernel_call(
        forward_kernel,
        [
            (PADDED, F32),
            ((CELLS, WIDTH), F32),
            ((CELLS, 1), F32),
            ((2, CELLS, PART), BF16),
            ((WIDTH, CELLS), BF16),
            ((2, CELLS, PART), BF16),
            ((WIDTH, CELLS), BF16),
        ],
        [pltpu.VMEM((CELLS, WIDTH), F32), pltpu.VMEM(SHIFTED, F32)],
        "forward",
        pl.CostEstimate(flops=8_000_000, bytes_accessed=2_000_000, transcendentals=256),
    )(tokens, low, high, dw_kernel, vectors, upstream)
    mine, theirs, block_out, mixed_grad = kernel_call(
        main_kernel,
        [
            ((PEERS, 40, 128), F32),
            ((PEERS, 40, 128), BF16),
            ((ROWS, COLS, WIDTH), BF16),
            ((ROWS, COLS, WIDTH), BF16),
        ],
        [
            pltpu.VMEM((64, WIDTH), F32),
            pltpu.VMEM((ROWS, COLS + 2 * MARGIN, WIDTH), F32),
            pltpu.VMEM((PEERS, 40, 128), F32),
        ],
        "main",
        pl.CostEstimate(flops=500_000_000, bytes_accessed=4_000_000, transcendentals=400_000),
    )(
        own, other, tokens, upstream, padded, normed, inv_std, norm_halves, norm_t, up_halves,
        up_t, vectors,
    )
    sums = (mine + other_core(theirs).astype(F32)).astype(BF16)
    sums, mixed_grad = lax.optimization_barrier((sums, mixed_grad))
    arrived = exchange(sums, ("y", "space"))
    grad_low, grad_high = neighbours(mixed_grad)
    arrived, grad_low, grad_high = lax.optimization_barrier((arrived, grad_low, grad_high))
    (column,) = kernel_call(middle_kernel, [((DEPTH, 8, PART), BF16)], name="middle")(arrived)
    column = exchange(column, "z", "z_back")
    (grad_tokens,) = kernel_call(
        backward_kernel,
        [((ROWS, COLS, WIDTH), BF16)],
        [pltpu.VMEM(PADDED, F32), pltpu.VMEM(SHIFTED, F32)],
        "backward",
        pl.CostEstimate(flops=8_000_000, bytes_accessed=1_000_000, transcendentals=0),
    )(mixed_grad, grad_low, grad_high, dw_kernel, upstream)
    height = lax.rem(lax.axis_index("y") + (HEIGHT - FIRST_Y), HEIGHT).reshape(1)
    column, grad_tokens, height = lax.optimization_barrier((column, grad_tokens, height))
    (spread,) = kernel_call(spread_kernel, [((PEERS, 8, PART), BF16)], name="spread")(column)
    done = exchange(spread, ("y", "space"))
    kernel_grad, gain_grad, shift_grad, scale_grad, grad_expand, grad_reduce = pl.pallas_call(
        final_kernel,
        out_shape=[
            jax.ShapeDtypeStruct(shape, F32)
            for shape in [(TAPS, TAPS, WIDTH)] + [(1, WIDTH)] * 3 + [(UNITS, WIDTH)] * 2
        ],
        in_specs=[
            pl.BlockSpec(memory_space=pltpu.SMEM),
            pl.BlockSpec(memory_space=pltpu.VMEM),
        ],
        compiler_params=pltpu.CompilerParams(vmem_limit_bytes=40 * 2**20),
        name="final",
    )(height, done)
    return (
        block_out[None],
        grad_tokens[None],
        kernel_grad,
        gain_grad[0],
        shift_grad[0],
        grad_expand,
        grad_reduce,
        scale_grad[0],
    )


def solution(mesh):
    grid = Mesh(mesh.devices.reshape(DEPTH, HEIGHT, CORES, QUARTERS), DP + ("space",))
    tokens, units = P(DP, "space", None, None), P(DP, None)
    in_specs = (tokens, P(), P(), P(), units, units, P(), tokens)
    out_specs = (tokens, tokens, P(), P(), P(), units, units, P())
    return jax.shard_map(shards, mesh=grid, in_specs=in_specs, out_specs=out_specs, check_vma=False)
```

```python
import jax
import jax.numpy as jnp
from jax import lax
from jax.experimental import pallas as pl
from jax.experimental.pallas import tpu as pltpu
from jax.sharding import Mesh, PartitionSpec as P

DEPTH, HEIGHT, CORES, QUARTERS = 16, 8, 2, 4
DP = ("z", "y", "core")
PEERS = HEIGHT * QUARTERS
ROWS, COLS, WIDTH, TAPS = 4, 64, 192, 7
CELLS = ROWS * COLS
HALO = TAPS // 2
PART = WIDTH // 2
UNITS = 3
HALF = HEIGHT * DEPTH * UNITS
BLOCK = DEPTH * UNITS
MARGIN = 8
F32, BF16 = jnp.float32, jnp.bfloat16
SMALL_ROWS = 4
FIRST_Z, LAST_Z, FIRST_Y, FIRST_X = 14, 8, 4, 2
PADDED = (ROWS + 2 * HALO, COLS + 2 * MARGIN, WIDTH)
SHIFTED = (TAPS, ROWS, COLS + 2 * MARGIN, WIDTH)


def kernel_call(body, outs, scratch=(), name=None, cost=None):
    return pl.pallas_call(
        body,
        out_shape=[jax.ShapeDtypeStruct(shape, kind) for shape, kind in outs],
        scratch_shapes=list(scratch),
        compiler_params=pltpu.CompilerParams(vmem_limit_bytes=40 * 2**20),
        name=name,
        cost_estimate=cost,
    )


def dot(a, b):
    return jnp.dot(a, b, preferred_element_type=F32)


def dot_rows(a, b):
    return lax.dot_general(a, b, (((0,), (0,)), ((), ())), preferred_element_type=F32)


def fill_padded(padded, low, block, high):
    padded[:, :MARGIN, :] = jnp.zeros((ROWS + 2 * HALO, MARGIN, WIDTH), F32)
    padded[:, MARGIN + COLS :, :] = jnp.zeros((ROWS + 2 * HALO, MARGIN, WIDTH), F32)
    inside = slice(MARGIN, MARGIN + COLS)
    padded[:HALO, inside, :] = low[...].astype(F32)
    padded[HALO : HALO + ROWS, inside, :] = block[...].astype(F32)
    padded[HALO + ROWS :, inside, :] = high[...].astype(F32)


def convolve(padded, shifted, tap, finish):
    for b in range(TAPS):
        taps_b = [jnp.broadcast_to(tap(a, b), (8, WIDTH)) for a in range(TAPS)]
        for t in range((MARGIN - HALO + b) // 8, (MARGIN - HALO + b + COLS + 7) // 8):
            acc = [None] * ROWS
            for i in range(ROWS + 2 * HALO):
                field = padded[i, 8 * t : 8 * t + 8, :]
                for r in range(ROWS):
                    if 0 <= i - r < TAPS:
                        term = field * taps_b[i - r]
                        acc[r] = term if acc[r] is None else acc[r] + term
            for r in range(ROWS):
                shifted[b, r, 8 * t : 8 * t + 8, :] = acc[r]
    for r in range(ROWS):
        for start in range(0, COLS, 32):
            total = None
            for b in range(TAPS):
                first = MARGIN - HALO + b + start
                value = shifted[b, r, first : first + 32, :]
                total = value if total is None else total + value
            finish(r, start, 32, total)


def forward_kernel(
    tokens, low, high, taps, vectors, cotangent,
    padded, normed, inv_std, norm_halves, norm_t, up_halves, up_t, mixed, shifted,
):
    fill_padded(padded, low, tokens, high)

    def finish(r, start, chunk, value):
        mixed[r * COLS + start : r * COLS + start + chunk, :] = value

    convolve(padded, shifted, lambda a, b: taps[a, b : b + 1, :], finish)
    value = mixed[...]
    centre = value - jnp.mean(value, -1, keepdims=True)
    inv = lax.rsqrt(jnp.mean(centre * centre, -1, keepdims=True) + 1e-06)
    norm = centre * inv
    normed[...] = norm
    inv_std[...] = inv
    rounded = (norm * vectors[0:1] + vectors[1:2]).astype(BF16)
    upstream = (cotangent[...].reshape(CELLS, WIDTH).astype(F32) * vectors[2:3]).astype(BF16)
    for h in range(2):
        norm_halves[h] = rounded[:, h * PART : (h + 1) * PART]
        up_halves[h] = upstream[:, h * PART : (h + 1) * PART]
    norm_t[...] = rounded.T
    up_t[...] = upstream.T


def main_kernel(
    own, other, cotangent, padded, normed, inv_std, norm_halves, norm_t, up_halves, up_t,
    vectors, mine, theirs_bf, branch_out, mixed_grad, smalls, grad_rows, theirs,
):
    branch = jnp.zeros((CELLS, WIDTH), F32)
    normed_grad = jnp.zeros((CELLS, WIDTH), F32)
    for weights, out in ((other, theirs), (own, mine)):
        expand, reduce = weights[:, :WIDTH], weights[:, WIDTH:]
        pre = dot(expand, norm_t[...])
        hidden_grad = dot(reduce, up_t[...])
        cumulative = 0.5 * (1.0 + lax.erf(pre * 0.7071067811865476))
        hidden = (pre * cumulative).astype(BF16)
        slope = cumulative + pre * jnp.exp(-0.5 * pre * pre) * 0.3989422804014327
        pre_grad = (hidden_grad * slope).astype(BF16)
        for q in range(QUARTERS):
            left, right = (pre_grad, norm_halves) if q < 2 else (hidden, up_halves)
            grad = dot(left, right[q % 2])
            for y in range(HEIGHT):
                base = y * BLOCK
                piece = y * QUARTERS + q
                out[piece, 0:40, 0:PART] = grad[base : base + 40]
                tail = grad[base + 40 : base + 48]
                for k in range(3):
                    out[piece, 8 * k : 8 * k + 8, PART:128] = tail[:, 32 * k : 32 * k + 32]
        branch += dot_rows(hidden, reduce)
        normed_grad += dot_rows(pre_grad, expand)
    branch_out[...] = branch
    norm = normed[...]
    upstream = cotangent[...].reshape(CELLS, WIDTH).astype(F32)
    smalls[TAPS * TAPS :, :] = jnp.zeros((64 - TAPS * TAPS, WIDTH), F32)
    smalls[49:50, :] = jnp.sum(normed_grad * norm, 0, keepdims=True)
    smalls[50:51, :] = jnp.sum(normed_grad, 0, keepdims=True)
    smalls[51:52, :] = jnp.sum(upstream * branch, 0, keepdims=True)
    scaled = normed_grad * vectors[0:1]
    grad = inv_std[...] * (
        scaled
        - jnp.mean(scaled, -1, keepdims=True)
        - norm * jnp.mean(scaled * norm, -1, keepdims=True)
    )
    grad_rows[:, :MARGIN, :] = jnp.zeros((ROWS, MARGIN, WIDTH), F32)
    grad_rows[:, MARGIN + COLS :, :] = jnp.zeros((ROWS, MARGIN, WIDTH), F32)
    grad_rows[:, MARGIN : MARGIN + COLS, :] = grad.reshape(ROWS, COLS, WIDTH)
    mixed_grad[...] = grad.astype(BF16).reshape(ROWS, COLS, WIDTH)
    for b in range(TAPS):
        acc = [None] * TAPS
        for t in range((MARGIN - HALO + b) // 8, (MARGIN - HALO + b + COLS + 7) // 8):
            first = 8 * t + HALO - b
            grads = [grad_rows[r, first : first + 8, :] for r in range(ROWS)]
            for i in range(ROWS + 2 * HALO):
                field = padded[i, 8 * t : 8 * t + 8, :]
                for r in range(ROWS):
                    a = i - r
                    if 0 <= a < TAPS:
                        term = field * grads[r]
                        acc[a] = term if acc[a] is None else acc[a] + term
        for a in range(TAPS):
            row = a * TAPS + b
            smalls[row : row + 1, :] = jnp.sum(acc[a], 0, keepdims=True)
    for piece in range(PEERS):
        row = SMALL_ROWS * (piece % 16)
        lane = PART * (piece // 16)
        values = smalls[row : row + SMALL_ROWS, lane : lane + PART]
        for out in (mine, theirs):
            for k in range(3):
                at = 24 + SMALL_ROWS * k
                out[piece, at : at + SMALL_ROWS, PART:128] = values[:, 32 * k : 32 * k + 32]
            out[piece, 36:40, PART:128] = jnp.zeros((4, 32), F32)
    theirs_bf[...] = theirs[...].astype(BF16)


def middle_kernel(arrived, column):
    total = arrived[0].astype(F32)
    for p in range(1, PEERS):
        total += arrived[p].astype(F32)
    tail = jnp.concatenate([total[8 * k : 8 * k + 8, PART:128] for k in range(3)], 1)
    grad = jnp.concatenate([total[:, :PART], tail], 0)
    at = [24 + SMALL_ROWS * k for k in range(3)]
    small = jnp.concatenate([total[i : i + SMALL_ROWS, PART:128] for i in at], 1)
    blank = jnp.zeros((1, PART), F32)
    for z in range(DEPTH):
        rows = [grad[z * UNITS : (z + 1) * UNITS], small, blank]
        column[(z + FIRST_Z - LAST_Z) % DEPTH] = jnp.concatenate(rows, 0).astype(BF16)


def spread_kernel(arrived, copies):
    total = jnp.sum(arrived[...].astype(F32), 0).astype(BF16)
    for p in range(PEERS):
        copies[p] = total


def final_kernel(height, done, kernel_grad, gain_grad, shift_grad, scale_grad, expand, reduce):
    y = height[0]
    for q in range(QUARTERS):
        out = expand if q < 2 else reduce
        block = done[y * QUARTERS + q].astype(F32)
        out[:, (q % 2) * PART : (q % 2 + 1) * PART] = block[0:UNITS]
    for p in range((TAPS * TAPS + 3 + SMALL_ROWS - 1) // SMALL_ROWS):
        block = jnp.concatenate([done[p].astype(F32), done[16 + p].astype(F32)], 1)
        for i in range(SMALL_ROWS):
            row = SMALL_ROWS * p + i
            value = block[UNITS + i : UNITS + i + 1]
            if row < TAPS * TAPS:
                kernel_grad[row // TAPS, row % TAPS : row % TAPS + 1, :] = value
            else:
                (gain_grad, shift_grad, scale_grad)[row - TAPS * TAPS][...] = value


def backward_kernel(
    grad, low, high, taps, cotangent, tokens, branch, vectors, out, block_out, padded, shifted
):
    flat = tokens[...].reshape(CELLS, WIDTH).astype(F32)
    total = flat + vectors[2:3] * branch[...]
    block_out[...] = total.astype(BF16).reshape(ROWS, COLS, WIDTH)
    fill_padded(padded, low, grad, high)

    def finish(r, start, chunk, value):
        upstream = cotangent[r, start : start + chunk, :].astype(F32)
        out[r, start : start + chunk, :] = (upstream + value).astype(BF16)

    def tap(a, b):
        return taps[TAPS - 1 - a, TAPS - 1 - b : TAPS - b, :]

    convolve(padded, shifted, tap, finish)


def neighbours(block):
    forward = [(i, i + 1) for i in range(QUARTERS - 1)]
    backward = [(target, source) for source, target in forward]
    low = lax.ppermute(block[ROWS - HALO :], "space", forward)
    high = lax.ppermute(block[:HALO], "space", backward)
    return low, high


def other_core(x):
    return lax.ppermute(x, "core", [(0, 1), (1, 0)])


def turned(count, first):
    return [(i + first) % count for i in range(count)]


ORDERS = {
    "z": turned(DEPTH, FIRST_Z),
    "z_back": turned(DEPTH, LAST_Z),
    "y": turned(HEIGHT, FIRST_Y),
    ("y", "space"): [
        y * QUARTERS + x for y in turned(HEIGHT, FIRST_Y) for x in turned(QUARTERS, FIRST_X)
    ],
}


def exchange(x, axes, order=None):
    groups = [ORDERS[order or axes]]
    return lax.all_to_all(x, axes, 0, 0, axis_index_groups=groups, tiled=True)


def shards(
    pressure_tokens, dw_kernel, norm_gain, norm_shift, w_expand, w_reduce, layer_scale, cotangent
):
    tokens, upstream = pressure_tokens[0], cotangent[0]

    def copies(x):
        return jnp.broadcast_to(x[None], (DEPTH,) + x.shape)

    column = exchange(jnp.concatenate([copies(w_expand), copies(w_reduce)], 2), "z")
    low, high = neighbours(tokens)
    vectors = jnp.stack([norm_gain, norm_shift, layer_scale])
    column, low, high, vectors = lax.optimization_barrier((column, low, high, vectors))
    plane = column.reshape(1, BLOCK, 2 * WIDTH)
    own = exchange(jnp.broadcast_to(plane, (HEIGHT, BLOCK, 2 * WIDTH)), "y")
    own, low = lax.optimization_barrier((own.reshape(HALF, 2 * WIDTH), low))
    other = other_core(own)
    padded, normed, inv_std, norm_halves, norm_t, up_halves, up_t = kernel_call(
        forward_kernel,
        [
            (PADDED, F32),
            ((CELLS, WIDTH), F32),
            ((CELLS, 1), F32),
            ((2, CELLS, PART), BF16),
            ((WIDTH, CELLS), BF16),
            ((2, CELLS, PART), BF16),
            ((WIDTH, CELLS), BF16),
        ],
        [pltpu.VMEM((CELLS, WIDTH), F32), pltpu.VMEM(SHIFTED, F32)],
        "forward",
        pl.CostEstimate(flops=8_000_000, bytes_accessed=2_000_000, transcendentals=256),
    )(tokens, low, high, dw_kernel, vectors, upstream)
    mine, theirs, branch, mixed_grad = kernel_call(
        main_kernel,
        [
            ((PEERS, 40, 128), F32),
            ((PEERS, 40, 128), BF16),
            ((CELLS, WIDTH), F32),
            ((ROWS, COLS, WIDTH), BF16),
        ],
        [
            pltpu.VMEM((64, WIDTH), F32),
            pltpu.VMEM((ROWS, COLS + 2 * MARGIN, WIDTH), F32),
            pltpu.VMEM((PEERS, 40, 128), F32),
        ],
        "main",
        pl.CostEstimate(flops=500_000_000, bytes_accessed=4_000_000, transcendentals=400_000),
    )(
        own, other, upstream, padded, normed, inv_std, norm_halves, norm_t, up_halves,
        up_t, vectors,
    )
    sums = (mine + other_core(theirs).astype(F32)).astype(BF16)
    sums, mixed_grad = lax.optimization_barrier((sums, mixed_grad))
    arrived = exchange(sums, ("y", "space"))
    grad_low, grad_high = neighbours(mixed_grad)
    arrived, grad_low, grad_high = lax.optimization_barrier((arrived, grad_low, grad_high))
    (column,) = kernel_call(middle_kernel, [((DEPTH, 8, PART), BF16)], name="middle")(arrived)
    column = exchange(column, "z", "z_back")
    grad_tokens, block_out = kernel_call(
        backward_kernel,
        [((ROWS, COLS, WIDTH), BF16)] * 2,
        [pltpu.VMEM(PADDED, F32), pltpu.VMEM(SHIFTED, F32)],
        "backward",
        pl.CostEstimate(flops=8_000_000, bytes_accessed=1_000_000, transcendentals=0),
    )(mixed_grad, grad_low, grad_high, dw_kernel, upstream, tokens, branch, vectors)
    height = lax.rem(lax.axis_index("y") + (HEIGHT - FIRST_Y), HEIGHT).reshape(1)
    column, grad_tokens, height = lax.optimization_barrier((column, grad_tokens, height))
    (spread,) = kernel_call(spread_kernel, [((PEERS, 8, PART), BF16)], name="spread")(column)
    done = exchange(spread, ("y", "space"))
    kernel_grad, gain_grad, shift_grad, scale_grad, grad_expand, grad_reduce = pl.pallas_call(
        final_kernel,
        out_shape=[
            jax.ShapeDtypeStruct(shape, F32)
            for shape in [(TAPS, TAPS, WIDTH)] + [(1, WIDTH)] * 3 + [(UNITS, WIDTH)] * 2
        ],
        in_specs=[
            pl.BlockSpec(memory_space=pltpu.SMEM),
            pl.BlockSpec(memory_space=pltpu.VMEM),
        ],
        compiler_params=pltpu.CompilerParams(vmem_limit_bytes=40 * 2**20),
        name="final",
    )(height, done)
    return (
        block_out[None],
        grad_tokens[None],
        kernel_grad,
        gain_grad[0],
        shift_grad[0],
        grad_expand,
        grad_reduce,
        scale_grad[0],
    )


def solution(mesh):
    grid = Mesh(mesh.devices.reshape(DEPTH, HEIGHT, CORES, QUARTERS), DP + ("space",))
    tokens, units = P(DP, "space", None, None), P(DP, None)
    in_specs = (tokens, P(), P(), P(), units, units, P(), tokens)
    out_specs = (tokens, tokens, P(), P(), P(), units, units, P())
    return jax.shard_map(shards, mesh=grid, in_specs=in_specs, out_specs=out_specs, check_vma=False)
```
